512 devices in a mesh: seq: 64 (over z, y), head: 8 (over x, core).
Axes of the slice: x: 4, y: 8, z: 8, core: 2. Of those that a mesh axis runs over, the one named last changes fastest.
Arguments:
- raw_keys: bfloat16 [2, 65536, 8, 128], P(None, 'seq', 'head'), may hold values from -6 to 6
- raw_values: bfloat16 [2, 65536, 8, 128], P(None, 'seq', 'head'), may hold values from -6 to 6
- phase: int32 [2], replicated, may hold values from 0 to 255, as said below
- ratio: int32 [2, 64], replicated, may hold values from 8 to 32, as said below
- resident_len: int32 [2, 64], replicated, may hold values from 1 to 256, as said below
- beacon_queries: bfloat16 [2, 8192, 8, 8, 128], P(None, 'seq', 'head'), may hold values from -150 to 150
- beacon_wk: bfloat16 [8192, 1024], P('seq', 'head'), may hold values from -0.125 to 0.125
- beacon_wv: bfloat16 [8192, 1024], P('seq', 'head'), may hold values from -0.125 to 0.125
- resident_keys: bfloat16 [2, 16384, 8, 128], P(None, 'seq', 'head'), may hold values from -6 to 6
- resident_values: bfloat16 [2, 16384, 8, 128], P(None, 'seq', 'head'), may hold values from -6 to 6
- decode_queries: bfloat16 [4, 2, 8, 8, 128], P(None, None, 'head'), may hold values from -150 to 150
- out_weight: bfloat16 [8192, 8192], P('head', 'seq'), may hold values from -0.0625 to 0.0625
Outputs:
- beacon_keys: bfloat16 [2, 8192, 8, 128], P(None, 'seq', 'head')
- beacon_values: bfloat16 [2, 8192, 8, 128], P(None, 'seq', 'head')
- projected: bfloat16 [4, 2, 8192], P(None, None, 'seq')
The draws below stay inside these ranges and needn't reach their ends.
Inputs may be any that keep to these rules, and one draw needn't show every extreme that they name: `phase`: some request has 255. `ratio`: each value is 1024 // 128 times 1, 2 or 4; both ends occur. `resident_len`: some pair has 256.
All inputs are finite; a program needn't handle non-finite values.
Results may differ from the reference program's by a relative error of at most 0.025.
Values may be sent and summed in bfloat16 or wider, within the bound.
No kernel may reach another device: no remote copies, remote signals or barrier semaphores. Data moves between devices by JAX's collectives and lax.ppermute only.
A program may use at most 64 MiB of HBM per device.

```python
import math
import jax
import jax.numpy as jnp
from jax import lax

KVH = 8
G = 8
HD = 128
D = 8192
INTERVAL = 1024
NB = 128
OFF = 256
REQ = 2
RES_DEV = 256
STEPS = 4
N_SEQ = 64


def draw_phase(key, part):
    base = jax.random.randint(key, (REQ,), 0, OFF)
    chosen = jax.random.randint(jax.random.fold_in(key, 7), (), 0, REQ)
    return jnp.where(jnp.arange(REQ) == chosen, OFF - 1, base).astype(jnp.int32)


def draw_ratio(key, part):
    power = jax.random.randint(key, (REQ, N_SEQ), 0, 3)
    flat_ids = jnp.arange(REQ * N_SEQ).reshape(REQ, N_SEQ)
    chosen = jax.random.randint(jax.random.fold_in(key, 3), (), 0, REQ * N_SEQ)
    power = jnp.where(flat_ids == chosen, 0, power)
    power = jnp.where(flat_ids == (chosen + 1) % (REQ * N_SEQ), 2, power)
    factor = jnp.where(power == 0, 1, jnp.where(power == 1, 2, 4))
    return (INTERVAL // NB * factor).astype(jnp.int32)


def draw_resident_len(key, part):
    base = jax.random.randint(key, (REQ, N_SEQ), 1, RES_DEV + 1)
    flat_ids = jnp.arange(REQ * N_SEQ).reshape(REQ, N_SEQ)
    chosen = jax.random.randint(jax.random.fold_in(key, 5), (), 0, REQ * N_SEQ)
    return jnp.where(flat_ids == chosen, RES_DEV, base).astype(jnp.int32)


def anchor_rows(key):
    anchors = jax.random.normal(jax.random.fold_in(key, 41), (REQ, N_SEQ, KVH, HD), jnp.float32)
    length = jnp.sqrt(jnp.sum(anchors * anchors, axis=-1, keepdims=True))
    anchors = anchors * (math.sqrt(HD) / length)
    return jnp.clip(anchors, -6.0, 6.0).astype(jnp.bfloat16).astype(jnp.float32)


def draw_resident_keys(key, part):
    whole = jax.random.normal(jax.random.fold_in(key, 42), (REQ, N_SEQ, RES_DEV, KVH, HD), jnp.float32)
    whole = jnp.clip(whole, -6.0, 6.0)
    whole = whole.at[:, :, 0].set(anchor_rows(key))
    return whole.reshape(REQ, N_SEQ * RES_DEV, KVH, HD).astype(jnp.bfloat16)


def draw_beacon_queries(key, part):
    inner = jax.random.fold_in(key, 21)
    shape = (REQ, N_SEQ * NB, KVH, G, HD)
    base = jax.random.normal(inner, shape, jnp.float32)
    return jnp.clip(2.0 * base, -12.0, 12.0).astype(jnp.bfloat16)


def draw_decode_queries(key, part):
    inner = jax.random.fold_in(key, 22)
    shape = (STEPS, REQ, KVH, G, HD)
    base = jax.random.normal(inner, shape, jnp.float32)
    return jnp.clip(2.5 * base, -12.0, 12.0).astype(jnp.bfloat16)


def steps_of(own_key, shape, split, smallest, high):
    level, own = 1.0, jax.random.fold_in(own_key, 6)
    for axis_at, shards_of in split:
        draws = jnp.exp(jax.random.uniform(jax.random.fold_in(own, axis_at), (shards_of,), jnp.float32, smallest / len(split), high / len(split)))
        level = level * jnp.repeat(draws, shape[axis_at] // shards_of).reshape([-1 if axis == axis_at else 1 for axis in range(len(shape))])
    return level


def noise(own_key, shape, spread, bound, pieces=(), kind=jnp.bfloat16):
    array = spread * jax.random.normal(own_key, shape, jnp.float32)
    if pieces:
        array = array * steps_of(own_key, shape, pieces, -0.22, 0.18)
    return jnp.clip(array, -bound, bound).astype(kind)


def setup_inputs(seed: int = 0) -> dict:
    key_list = jax.random.split(jax.random.key(seed), 13)
    raw_keys = noise(key_list[0], (REQ, INTERVAL * N_SEQ, KVH, HD), 1.0, 6.0, ((1, 64), (2, 8)))
    raw_values = noise(key_list[1], (REQ, INTERVAL * N_SEQ, KVH, HD), 1.0, 6.0, ((1, 64), (2, 8)))
    phase = draw_phase(jax.random.fold_in(key_list[12], 71), 0)
    ratio = draw_ratio(jax.random.fold_in(key_list[12], 71), 0)
    resident_len = draw_resident_len(jax.random.fold_in(key_list[12], 71), 0)
    beacon_queries = draw_beacon_queries(jax.random.fold_in(key_list[12], 71), 0)
    beacon_wk = noise(key_list[6], (D, KVH * HD), (D // 4) ** -0.5, 0.125, ((0, 64), (1, 8)))
    beacon_wv = noise(key_list[7], (D, KVH * HD), (D // 4) ** -0.5, 0.125, ((0, 64), (1, 8)))
    resident_keys = draw_resident_keys(jax.random.fold_in(key_list[12], 71), 0)
    resident_values = noise(key_list[9], (REQ, N_SEQ * RES_DEV, KVH, HD), 1.0, 6.0, ((1, 64), (2, 8)))
    decode_queries = draw_decode_queries(jax.random.fold_in(key_list[12], 71), 0)
    out_weight = noise(key_list[11], (D, D), D ** -0.5, 0.0625, ((0, 8), (1, 64)))
    return dict(raw_keys=raw_keys, raw_values=raw_values, phase=phase, ratio=ratio, resident_len=resident_len, beacon_queries=beacon_queries, beacon_wk=beacon_wk, beacon_wv=beacon_wv, resident_keys=resident_keys, resident_values=resident_values, decode_queries=decode_queries, out_weight=out_weight)


masked_score = -1e+30

def reference(raw_keys, raw_values, phase, ratio, resident_len, beacon_queries, beacon_wk, beacon_wv, resident_keys, resident_values, decode_queries, out_weight):
    requests = raw_keys.shape[0]
    heads = raw_keys.shape[2]
    inv_root = 1.0 / math.sqrt(HD)
    shaped_keys = raw_keys.reshape(requests, N_SEQ, INTERVAL, heads, HD)
    shaped_values = raw_values.reshape(requests, N_SEQ, INTERVAL, heads, HD)
    tails_k = shaped_keys[:, :, INTERVAL - OFF:]
    tails_v = shaped_values[:, :, INTERVAL - OFF:]
    near_keys = jnp.concatenate([jnp.zeros_like(tails_k[:, :1]), tails_k[:, :-1]], axis=1)
    near_values = jnp.concatenate([jnp.zeros_like(tails_v[:, :1]), tails_v[:, :-1]], axis=1)
    window_keys = jnp.moveaxis(jnp.concatenate([near_keys, shaped_keys], axis=2), 1, 0)
    window_values = jnp.moveaxis(jnp.concatenate([near_values, shaped_values], axis=2), 1, 0)
    queries = jnp.moveaxis(beacon_queries.reshape(requests, N_SEQ, NB, heads, G, HD), 1, 0)
    slot_ids = jnp.arange(NB, dtype=jnp.int32)
    row_ids = jnp.arange(OFF + INTERVAL, dtype=jnp.int32)
    key_map = beacon_wk.astype(jnp.float32)
    value_map = beacon_wv.astype(jnp.float32)

    def per_shard(members):
        shard_index, query_block, key_rows, value_rows, shard_ratio = members
        positions = row_ids[None, :] - OFF + phase[:, None]
        present = (shard_index > 0) | (positions >= phase[:, None])
        lead_in = jnp.where(shard_index == 0, phase, 0)
        reaches = (slot_ids[None, :] + 1) * shard_ratio[:, None] + lead_in[:, None]
        allowed = present[:, None, :] & (positions >= 0)[:, None, :] & (positions < INTERVAL)[:, None, :] & (positions[:, None, :] < reaches[:, :, None])
        scores = jnp.einsum('rjkgd,rikd->rjkgi', query_block.astype(jnp.float32), key_rows.astype(jnp.float32)) * inv_root
        cache_mask = allowed[:, :, None, None, :]
        row_peak = lax.optimization_barrier(jnp.max(jnp.where(cache_mask, scores, masked_score), axis=-1, keepdims=True))
        weights = jnp.where(cache_mask, jnp.exp(scores - row_peak), 0.0)
        weight_sum = lax.optimization_barrier(jnp.sum(weights, axis=-1))
        rounded = lax.optimization_barrier(weights.astype(jnp.bfloat16))
        weighted = jnp.einsum('rjkgi,rikd->rjkgd', rounded.astype(jnp.float32), value_rows.astype(jnp.float32))
        pooled = lax.optimization_barrier((weighted / weight_sum[..., None]).astype(jnp.bfloat16))
        pooled_flat = pooled.reshape(requests, NB, heads * G * HD).astype(jnp.float32)
        made_keys = jnp.einsum('rjx,xy->rjy', pooled_flat, key_map).reshape(requests, NB, heads, HD)
        made_values = jnp.einsum('rjx,xy->rjy', pooled_flat, value_map).reshape(requests, NB, heads, HD)
        slot_live = (slot_ids[None, :] < (INTERVAL // shard_ratio)[:, None])[:, :, None, None]
        return (jnp.where(slot_live, made_keys, 0.0).astype(jnp.bfloat16), jnp.where(slot_live, made_values, 0.0).astype(jnp.bfloat16))
    made_k, made_v = lax.map(per_shard, (jnp.arange(N_SEQ, dtype=jnp.int32), queries, window_keys, window_values, jnp.transpose(ratio)))
    beacon_keys = jnp.moveaxis(made_k, 0, 1).reshape(requests, N_SEQ * NB, heads, HD)
    beacon_values = jnp.moveaxis(made_v, 0, 1).reshape(requests, N_SEQ * NB, heads, HD)
    leftover_keys = shaped_keys[:, N_SEQ - 1, INTERVAL - OFF:]
    leftover_values = shaped_values[:, N_SEQ - 1, INTERVAL - OFF:]
    cache_keys = jnp.concatenate([resident_keys, beacon_keys, leftover_keys], axis=1)
    cache_values = jnp.concatenate([resident_values, beacon_values, leftover_values], axis=1)
    resident_ok = (jnp.arange(RES_DEV, dtype=jnp.int32)[None, None, :] < resident_len[:, :, None]).reshape(requests, N_SEQ * RES_DEV)
    beacon_ok = (slot_ids[None, None, :] < (INTERVAL // ratio)[:, :, None]).reshape(requests, N_SEQ * NB)
    leftover_ok = jnp.arange(OFF, dtype=jnp.int32)[None, :] >= OFF - phase[:, None]
    usable = jnp.concatenate([resident_ok, beacon_ok, leftover_ok], axis=1)
    scores = jnp.einsum('srkgd,rikd->rksgi', decode_queries.astype(jnp.float32), cache_keys.astype(jnp.float32)) * inv_root
    cache_mask = usable[:, None, None, None, :]
    row_peak = lax.optimization_barrier(jnp.max(jnp.where(cache_mask, scores, masked_score), axis=-1, keepdims=True))
    weights = jnp.where(cache_mask, jnp.exp(scores - row_peak), 0.0)
    weight_sum = lax.optimization_barrier(jnp.sum(weights, axis=-1))
    rounded = lax.optimization_barrier(weights.astype(jnp.bfloat16))
    weighted = jnp.einsum('rksgi,rikd->rksgd', rounded.astype(jnp.float32), cache_values.astype(jnp.float32))
    attended = (weighted / weight_sum[..., None]).astype(jnp.bfloat16)
    attended = jnp.transpose(attended, (2, 0, 1, 3, 4)).reshape(STEPS * requests, D)
    projected = jnp.dot(attended, out_weight, preferred_element_type=jnp.float32).astype(jnp.bfloat16)
    return (beacon_keys, beacon_values, projected.reshape(STEPS, requests, D))
```

```python
import math

import jax
import jax.numpy as jnp
from jax import lax
from jax.experimental import pallas as pl
from jax.experimental.pallas import tpu as pltpu
from jax.sharding import Mesh, PartitionSpec as P

G = 8
HD = 128
INTERVAL = 1024
NB = 128
OFF = 256
STEPS = 4
REQ = 2
RES = 256
ROWS = STEPS * REQ * G
SCALE = math.log2(math.e) / math.sqrt(HD)
MASKED = -1e30
SEQ = ("z", "y")
BF = jnp.bfloat16
F32 = jnp.float32


def dot_nt(a, b):
    return lax.dot_general(a, b, (((1,), (1,)), ((), ())), preferred_element_type=F32)


def dot_nn(a, b):
    return jnp.dot(a, b, preferred_element_type=F32)


def pool_kernel(par, q_ref, rk_ref, rv_ref, nk_ref, nv_ref, out_ref):
    r = pl.program_id(0)
    low, step, base, end = par[r, 0], par[r, 1], par[r, 2], par[r, 3]
    col = lax.broadcasted_iota(jnp.int32, (2 * NB, OFF + INTERVAL), 1)
    slot = lax.broadcasted_iota(jnp.int32, (2 * NB, OFF + INTERVAL), 0) % NB
    bound = jnp.minimum(base + (slot + 1) * step, end)
    allowed = (col >= low) & (col < bound)
    for pair in range(G // 2):
        q = q_ref[0, 2 * pair : 2 * pair + 2].reshape(2 * NB, HD)
        scores = jnp.concatenate([dot_nt(q, nk_ref[0]), dot_nt(q, rk_ref[0])], axis=1)
        scores = jnp.where(allowed, scores * SCALE, MASKED)
        peak = jnp.max(scores, axis=1, keepdims=True)
        weights = jnp.exp2(scores - peak)
        total = jnp.sum(weights, axis=1, keepdims=True)
        weights = weights.astype(BF)
        weighted = dot_nn(weights[:, :OFF], nv_ref[0]) + dot_nn(weights[:, OFF:], rv_ref[0])
        pooled = (weighted / total).astype(BF)
        for copy in range(4):
            for half in range(2):
                at = (2 * pair + half) * HD
                out_ref[copy, :, at : at + HD] = pooled[half * NB : (half + 1) * NB]


def pool(par, queries, raw_k, raw_v, near_k, near_v):
    return pl.pallas_call(
        pool_kernel,
        out_shape=jax.ShapeDtypeStruct((4, REQ * NB, G * HD), BF),
        grid_spec=pltpu.PrefetchScalarGridSpec(
            num_scalar_prefetch=1,
            grid=(REQ,),
            in_specs=[
                pl.BlockSpec((1, G, NB, HD), lambda r, par: (r, 0, 0, 0)),
                pl.BlockSpec((1, INTERVAL, HD), lambda r, par: (r, 0, 0)),
                pl.BlockSpec((1, INTERVAL, HD), lambda r, par: (r, 0, 0)),
                pl.BlockSpec((1, OFF, HD), lambda r, par: (r, 0, 0)),
                pl.BlockSpec((1, OFF, HD), lambda r, par: (r, 0, 0)),
            ],
            out_specs=pl.BlockSpec((4, NB, G * HD), lambda r, par: (0, r, 0)),
        ),
        compiler_params=pltpu.CompilerParams(vmem_limit_bytes=40 << 20),
        name="pool",
    )(par, queries, raw_k, raw_v, near_k, near_v)


def lanes():
    return lax.broadcasted_iota(jnp.int32, (ROWS, HD), 1)


def pieces(value):
    high = value.astype(BF).astype(F32)
    rest = value - high
    middle = rest.astype(BF).astype(F32)
    return high, middle, rest - middle


def pack(out_ref, weighted, peak, total):
    lane = lanes()
    extra = jnp.zeros((ROWS, HD), F32)
    for at, piece in enumerate(pieces(peak) + pieces(total)):
        extra = jnp.where(lane == at, piece, extra)
    weighted, extra = weighted.astype(BF), extra.astype(BF)
    for copy in range(out_ref.shape[0]):
        out_ref[copy, :, :HD] = weighted
        out_ref[copy, :, HD:] = extra


def merge(in_ref):
    lane = lanes()
    peaks, totals = [], []
    for i in range(in_ref.shape[0]):
        extra = in_ref[i, :, HD:].astype(F32)
        peaks.append(jnp.sum(jnp.where(lane < 3, extra, 0.0), axis=1, keepdims=True))
        totals.append(jnp.sum(jnp.where(lane >= 3, extra, 0.0), axis=1, keepdims=True))
    peak = peaks[0]
    for other in peaks[1:]:
        peak = jnp.maximum(peak, other)
    weighted, total = 0.0, 0.0
    for i in range(in_ref.shape[0]):
        factor = jnp.exp2(peaks[i] - peak)
        weighted += in_ref[i, :, :HD].astype(F32) * factor
        total += totals[i] * factor
    return weighted, peak, total


def decode_kernel(
    par, po_ref, pt_ref, wo_ref, wt_ref, q_ref, sk_ref, sv_ref, tk_ref, tv_ref, bk_ref, bv_ref, out_ref, acc
):
    step = pl.program_id(0)
    part = dot_nn(po_ref[0], wo_ref[...]) + dot_nn(pt_ref[0], wt_ref[...])

    @pl.when(step == 0)
    def _():
        acc[...] = part

    @pl.when(step > 0)
    def _():
        acc[...] += part

    @pl.when(step == 3)
    def _():
        queries = q_ref[...]
        of_row = lax.broadcasted_iota(jnp.int32, (ROWS, RES), 0) % REQ
        col = lax.broadcasted_iota(jnp.int32, (ROWS, RES), 1)
        row = lax.broadcasted_iota(jnp.int32, (NB, HD), 0)
        keys, values, usable = [], [], []
        for r in range(REQ):
            made = jnp.where((row < par[r, 0])[:, :1], acc[r * NB : (r + 1) * NB], 0.0).astype(BF)
            bk_ref[r] = made[:, :HD]
            bv_ref[r] = made[:, HD:]
            keys += [sk_ref[r], tk_ref[r], made[:, :HD]]
            values += [sv_ref[r], tv_ref[r], made[:, HD:]]
            mine = of_row == r
            usable += [
                mine & (col < par[r, 1]),
                mine & (col >= par[r, 2]),
                (mine & (col < par[r, 0]))[:, :NB],
            ]
        scores = [
            jnp.where(ok, dot_nt(queries, k) * SCALE, MASKED) for k, ok in zip(keys, usable)
        ]
        scores = jnp.concatenate(scores, axis=1)
        peak = jnp.max(scores, axis=1, keepdims=True)
        weights = jnp.exp2(scores - peak)
        total = jnp.sum(weights, axis=1, keepdims=True)
        weights = weights.astype(BF)
        weighted, at = 0.0, 0
        for v in values:
            weighted += dot_nn(weights[:, at : at + v.shape[0]], v)
            at += v.shape[0]
        pack(out_ref, weighted, peak, total)


def project_decode(par, p_own, p_other, weights, queries, res_k, res_v, raw_k, raw_v):
    whole = lambda i, par: (0, 0, 0)
    return pl.pallas_call(
        decode_kernel,
        out_shape=(
            jax.ShapeDtypeStruct((REQ, NB, HD), BF),
            jax.ShapeDtypeStruct((REQ, NB, HD), BF),
            jax.ShapeDtypeStruct((8, ROWS, 2 * HD), BF),
        ),
        grid_spec=pltpu.PrefetchScalarGridSpec(
            num_scalar_prefetch=1,
            grid=(4,),
            in_specs=[
                pl.BlockSpec((1, REQ * NB, G * HD), lambda i, par: (i, 0, 0)),
                pl.BlockSpec((1, REQ * NB, G * HD), lambda i, par: (i, 0, 0)),
                pl.BlockSpec((G * HD, 2 * HD), lambda i, par: (2 * i + par[2, 0], 0)),
                pl.BlockSpec((G * HD, 2 * HD), lambda i, par: (2 * i + 1 - par[2, 0], 0)),
                pl.BlockSpec((ROWS, HD), lambda i, par: (0, 0)),
                pl.BlockSpec((REQ, RES, HD), whole),
                pl.BlockSpec((REQ, RES, HD), whole),
                pl.BlockSpec((REQ, OFF, HD), lambda i, par: (0, INTERVAL // OFF - 1, 0)),
                pl.BlockSpec((REQ, OFF, HD), lambda i, par: (0, INTERVAL // OFF - 1, 0)),
            ],
            out_specs=[
                pl.BlockSpec((REQ, NB, HD), whole),
                pl.BlockSpec((REQ, NB, HD), whole),
                pl.BlockSpec((8, ROWS, 2 * HD), whole),
            ],
            scratch_shapes=[pltpu.VMEM((REQ * NB, 2 * HD), F32)],
        ),
        compiler_params=pltpu.CompilerParams(vmem_limit_bytes=40 << 20),
        name="project_decode",
    )(par, p_own, p_other, weights, weights, queries, res_k, res_v, raw_k, raw_v)


def combine_kernel(in_ref, out_ref):
    pack(out_ref, *merge(in_ref))


def combine(state):
    return pl.pallas_call(
        combine_kernel, out_shape=jax.ShapeDtypeStruct((8, ROWS, 2 * HD), BF), name="combine"
    )(state)


def attend_kernel(in_ref, w_ref, out_ref):
    weighted, _, total = merge(in_ref)
    attended = weighted / total
    rows = STEPS * REQ
    flat = jnp.concatenate([attended[g * rows : (g + 1) * rows] for g in range(G)], axis=1)
    part = dot_nn(flat.astype(BF), w_ref[...])
    for copy in range(8):
        out_ref[copy] = part


def attend(state, out_weight):
    return pl.pallas_call(
        attend_kernel,
        out_shape=jax.ShapeDtypeStruct((8, STEPS * REQ, HD), F32),
        name="attend",
    )(state, out_weight)


def body(
    raw_keys,
    raw_values,
    phase,
    ratio,
    resident_len,
    beacon_queries,
    beacon_wk,
    beacon_wv,
    resident_keys,
    resident_values,
    decode_queries,
    out_weight,
):
    shard = lax.axis_index(SEQ)
    count = lax.axis_size(SEQ)
    first, last = shard == 0, shard == count - 1
    weights = lax.all_gather(
        jnp.concatenate([beacon_wk, beacon_wv], axis=1), SEQ, axis=0, tiled=True
    )
    raw_k, raw_v = raw_keys[:, :, 0], raw_values[:, :, 0]
    tails = jnp.stack([raw_k[:, INTERVAL - OFF :], raw_v[:, INTERVAL - OFF :]])
    near = lax.ppermute(tails, SEQ, [(i, i + 1) for i in range(count - 1)])
    own_ratio = lax.dynamic_index_in_dim(ratio, shard, 1, keepdims=False)
    own_len = lax.dynamic_index_in_dim(resident_len, shard, 1, keepdims=False)
    lead = jnp.where(first, phase, 0)
    shift = OFF - phase
    pool_par = jnp.stack([lead + shift, own_ratio, lead + shift, shift + INTERVAL], axis=1)
    queries = jnp.transpose(beacon_queries[:, :, 0], (0, 2, 1, 3))
    pooled = pool(pool_par, queries, raw_k, raw_v, near[0], near[1])
    p_own = lax.all_to_all(pooled, "x", 0, 0)
    p_other = lax.ppermute(p_own, "c", [(0, 1), (1, 0)])
    live = INTERVAL // own_ratio
    leftover = jnp.where(last, shift, OFF)
    core = jnp.full((1, 3), lax.axis_index("c"), jnp.int32)
    decode_par = jnp.concatenate([jnp.stack([live, own_len, leftover], axis=1), core])
    step_queries = jnp.transpose(decode_queries[:, :, 0], (2, 0, 1, 3)).reshape(ROWS, HD)
    beacon_k, beacon_v, state = project_decode(
        decode_par,
        p_own,
        p_other,
        weights,
        step_queries,
        resident_keys[:, :, 0],
        resident_values[:, :, 0],
        raw_k,
        raw_v,
    )
    state = combine(lax.all_to_all(state, "y", 0, 0))
    parts = attend(lax.all_to_all(state, "z", 0, 0), out_weight)
    parts = lax.all_to_all(parts, ("x", "c"), 0, 0)
    projected = jnp.sum(parts, axis=0).astype(BF).reshape(STEPS, REQ, HD)
    return beacon_k[:, :, None], beacon_v[:, :, None], projected


def solution(mesh):
    fine = Mesh(mesh.devices.reshape(8, 8, 4, 2), ("z", "y", "x", "c"))
    head = ("x", "c")
    return jax.shard_map(
        body,
        mesh=fine,
        in_specs=(
            P(None, SEQ, head, None),
            P(None, SEQ, head, None),
            P(),
            P(),
            P(),
            P(None, SEQ, head, None, None),
            P(SEQ, head),
            P(SEQ, head),
            P(None, SEQ, head, None),
            P(None, SEQ, head, None),
            P(None, None, head, None, None),
            P(head, SEQ),
        ),
        out_specs=(
            P(None, SEQ, head, None),
            P(None, SEQ, head, None),
            P(None, None, SEQ),
        ),
        check_vma=False,
    )
```

```python
import math

import jax
import jax.numpy as jnp
from jax import lax
from jax.experimental import pallas as pl
from jax.experimental.pallas import tpu as pltpu
from jax.sharding import Mesh, PartitionSpec as P

G = 8
HD = 128
INTERVAL = 1024
NB = 128
OFF = 256
STEPS = 4
REQ = 2
RES = 256
ROWS = STEPS * REQ * G
SCALE = math.log2(math.e) / math.sqrt(HD)
MASKED = -1e30
SEQ = ("z", "y")
BF = jnp.bfloat16
F32 = jnp.float32


def dot_nt(a, b):
    return lax.dot_general(a, b, (((1,), (1,)), ((), ())), preferred_element_type=F32)


def dot_nn(a, b):
    return jnp.dot(a, b, preferred_element_type=F32)


def stage_kernel(wk_ref, wv_ref, tk_ref, tv_ref, w_ref, tails_ref):
    for copy in range(8):
        w_ref[copy, :, :HD] = wk_ref[...]
        w_ref[copy, :, HD:] = wv_ref[...]
    tails_ref[0] = tk_ref[...]
    tails_ref[1] = tv_ref[...]


def stage(wk, wv, raw_k, raw_v):
    tail = pl.BlockSpec((REQ, OFF, HD), lambda i: (0, INTERVAL // OFF - 1, 0))
    weight = pl.BlockSpec((HD, HD), lambda i: (0, 0))
    return pl.pallas_call(
        stage_kernel,
        out_shape=(
            jax.ShapeDtypeStruct((8, HD, 2 * HD), BF),
            jax.ShapeDtypeStruct((2, REQ, OFF, HD), BF),
        ),
        grid=(1,),
        in_specs=[weight, weight, tail, tail],
        out_specs=(
            pl.BlockSpec((8, HD, 2 * HD), lambda i: (0, 0, 0)),
            pl.BlockSpec((2, REQ, OFF, HD), lambda i: (0, 0, 0, 0)),
        ),
        name="stage",
    )(wk, wv, raw_k, raw_v)


def pool_kernel(at_ref, phase_ref, ratio_ref, q_ref, rk_ref, rv_ref, near_ref, out_ref):
    r = pl.program_id(0)
    shard = at_ref[0]
    phase, step = phase_ref[r], ratio_ref[r, shard]
    start = OFF - phase
    low = start + jnp.where(shard == 0, phase, 0)
    col = lax.broadcasted_iota(jnp.int32, (2 * NB, OFF + INTERVAL), 1)
    slot = lax.broadcasted_iota(jnp.int32, (2 * NB, OFF + INTERVAL), 0) % NB
    bound = jnp.minimum(low + (slot + 1) * step, start + INTERVAL)
    allowed = (col >= low) & (col < bound)
    for pair in range(G // 2):
        q = q_ref[0, 2 * pair : 2 * pair + 2].reshape(2 * NB, HD)
        scores = jnp.concatenate([dot_nt(q, near_ref[0, 0]), dot_nt(q, rk_ref[0])], axis=1)
        scores = jnp.where(allowed, scores * SCALE, MASKED)
        peak = jnp.max(scores, axis=1, keepdims=True)
        weights = jnp.exp2(scores - peak)
        total = jnp.sum(weights, axis=1, keepdims=True)
        weights = weights.astype(BF)
        weighted = dot_nn(weights[:, :OFF], near_ref[1, 0]) + dot_nn(weights[:, OFF:], rv_ref[0])
        pooled = (weighted / total).astype(BF)
        for copy in range(4):
            for half in range(2):
                at = (2 * pair + half) * HD
                out_ref[copy, :, at : at + HD] = pooled[half * NB : (half + 1) * NB]


def pool(at, phase, ratio, queries, raw_k, raw_v, near):
    return pl.pallas_call(
        pool_kernel,
        out_shape=jax.ShapeDtypeStruct((4, REQ * NB, G * HD), BF),
        grid_spec=pltpu.PrefetchScalarGridSpec(
            num_scalar_prefetch=3,
            grid=(REQ,),
            in_specs=[
                pl.BlockSpec((1, G, NB, HD), lambda r, *_: (r, 0, 0, 0)),
                pl.BlockSpec((1, INTERVAL, HD), lambda r, *_: (r, 0, 0)),
                pl.BlockSpec((1, INTERVAL, HD), lambda r, *_: (r, 0, 0)),
                pl.BlockSpec((2, 1, OFF, HD), lambda r, *_: (0, r, 0, 0)),
            ],
            out_specs=pl.BlockSpec((4, NB, G * HD), lambda r, *_: (0, r, 0)),
        ),
        compiler_params=pltpu.CompilerParams(vmem_limit_bytes=40 << 20),
        name="pool",
    )(at, phase, ratio, queries, raw_k, raw_v, near)


def pieces(value):
    high = value.astype(BF).astype(F32)
    rest = value - high
    middle = rest.astype(BF).astype(F32)
    return high, middle, rest - middle


def pack(out_ref, weighted, peak, total):
    row = lax.broadcasted_iota(jnp.int32, (16, HD), 0)
    extra = jnp.zeros((16, HD), F32)
    for at, piece in enumerate(pieces(peak) + pieces(total)):
        extra = jnp.where(row == at, piece, extra)
    weighted, extra = weighted.astype(BF), extra.astype(BF)
    for copy in range(out_ref.shape[0]):
        out_ref[copy, :ROWS] = weighted
        out_ref[copy, ROWS:] = extra


def merge(in_ref, divide):
    extra = in_ref[:, ROWS:, :].astype(F32)
    peaks = extra[:, 0] + extra[:, 1] + extra[:, 2]
    totals = extra[:, 3] + extra[:, 4] + extra[:, 5]
    peak = jnp.max(peaks, axis=0, keepdims=True)
    factors = jnp.exp2(peaks - peak)
    total = jnp.sum(totals * factors, axis=0, keepdims=True)
    scales = (factors / total if divide else factors).T
    weighted = 0.0
    for i in range(in_ref.shape[0]):
        weighted += in_ref[i, :ROWS].astype(F32) * scales[:ROWS, i : i + 1]
    return weighted, peak, total


def decode_kernel(
    at_ref, phase_ref, ratio_ref, len_ref,
    po_ref, pt_ref, w_ref, q_ref, sk_ref, sv_ref, rk_ref, rv_ref,
    bk_ref, bv_ref, out_ref, held, other, sems, other_sems,
):
    shard, core, last = at_ref[0], at_ref[1], at_ref[2]
    copies = [
        pltpu.make_async_copy(w_ref.at[pl.ds(k * G * HD, G * HD)], held.at[k], sems.at[k])
        for k in range(8)
    ]
    other_copies = [
        pltpu.make_async_copy(pt_ref.at[x], other.at[x], other_sems.at[x]) for x in range(4)
    ]
    for x in range(4):
        copies[2 * x].start()
        copies[2 * x + 1].start()
        other_copies[x].start()
    queries = q_ref[...]
    of_row = lax.broadcasted_iota(jnp.int32, (ROWS, RES), 0) % REQ
    col = lax.broadcasted_iota(jnp.int32, (ROWS, RES), 1)
    row = lax.broadcasted_iota(jnp.int32, (NB, 2 * HD), 0)
    live = [INTERVAL // ratio_ref[r, shard] for r in range(REQ)]

    def score(keys, usable):
        return jnp.where(usable, dot_nt(queries, keys) * SCALE, MASKED)

    early, late = [], []
    for r in range(REQ):
        mine = of_row == r
        leftover = jnp.where(last == 1, OFF - phase_ref[r], OFF)
        early.append(score(sk_ref[r], mine & (col < len_ref[r, shard])))
        early.append(score(rk_ref[r], mine & (col >= leftover)))
    total_part = 0.0
    for x in range(4):
        copies[2 * x].wait()
        copies[2 * x + 1].wait()
        other_copies[x].wait()
        total_part += dot_nn(po_ref[x], held[2 * x + core])
        total_part += dot_nn(other[x], held[2 * x + 1 - core])
    made = []
    for r in range(REQ):
        part = total_part[r * NB : (r + 1) * NB]
        made.append(jnp.where(row < live[r], part, 0.0).astype(BF))
        bk_ref[r] = made[r][:, :HD]
        bv_ref[r] = made[r][:, HD:]
        late.append(score(made[r][:, :HD], (of_row == r)[:, :NB] & (col[:, :NB] < live[r])))
    scores = jnp.concatenate(early + late, axis=1)
    peak = jnp.max(scores, axis=1, keepdims=True)
    weights = jnp.exp2(scores - peak)
    total = jnp.sum(weights, axis=1, keepdims=True)
    weights = weights.astype(BF)
    values = [sv_ref[0], rv_ref[0], sv_ref[1], rv_ref[1], made[0][:, HD:], made[1][:, HD:]]
    weighted, at = 0.0, 0
    for v in values:
        weighted += dot_nn(weights[:, at : at + v.shape[0]], v)
        at += v.shape[0]
    lane = lax.broadcasted_iota(jnp.int32, (ROWS, HD), 1)
    columns = jnp.where(lane == 0, peak, total)
    rows = jnp.concatenate([columns, jnp.zeros((HD - ROWS, HD), F32)], axis=0).T
    pack(out_ref, weighted, rows[0:1], rows[1:2])


def project_decode(at, phase, ratio, length, p_own, p_other, weights, queries, res_k, res_v, raw_k, raw_v):
    whole = lambda i, *_: (0, 0, 0)
    tail = pl.BlockSpec((REQ, OFF, HD), lambda i, *_: (0, INTERVAL // OFF - 1, 0))
    return pl.pallas_call(
        decode_kernel,
        out_shape=(
            jax.ShapeDtypeStruct((REQ, NB, HD), BF),
            jax.ShapeDtypeStruct((REQ, NB, HD), BF),
            jax.ShapeDtypeStruct((8, ROWS + 16, HD), BF),
        ),
        grid_spec=pltpu.PrefetchScalarGridSpec(
            num_scalar_prefetch=4,
            grid=(1,),
            in_specs=[
                pl.BlockSpec((4, REQ * NB, G * HD), whole),
                pl.BlockSpec(memory_space=pltpu.HBM),
                pl.BlockSpec(memory_space=pltpu.HBM),
                pl.BlockSpec((ROWS, HD), lambda i, *_: (0, 0)),
                pl.BlockSpec((REQ, RES, HD), whole),
                pl.BlockSpec((REQ, RES, HD), whole),
                tail,
                tail,
            ],
            out_specs=[
                pl.BlockSpec((REQ, NB, HD), whole),
                pl.BlockSpec((REQ, NB, HD), whole),
                pl.BlockSpec((8, ROWS + 16, HD), whole),
            ],
            scratch_shapes=[
                pltpu.VMEM((8, G * HD, 2 * HD), BF),
                pltpu.VMEM((4, REQ * NB, G * HD), BF),
                pltpu.SemaphoreType.DMA((8,)),
                pltpu.SemaphoreType.DMA((4,)),
            ],
        ),
        compiler_params=pltpu.CompilerParams(vmem_limit_bytes=40 << 20),
        name="project_decode",
    )(
        at,
        phase,
        ratio,
        length,
        p_own,
        pltpu.with_memory_space_constraint(p_other, pltpu.HBM),
        pltpu.with_memory_space_constraint(weights, pltpu.HBM),
        queries,
        res_k,
        res_v,
        raw_k,
        raw_v,
    )


def combine_kernel(in_ref, out_ref):
    pack(out_ref, *merge(in_ref, False))


def combine(state):
    return pl.pallas_call(
        combine_kernel, out_shape=pltpu.VMEM(state.shape, BF), name="combine"
    )(pltpu.with_memory_space_constraint(state, pltpu.VMEM))


def attend_kernel(in_ref, w_ref, out_ref):
    attended, _, _ = merge(in_ref, True)
    rows = STEPS * REQ
    flat = jnp.concatenate([attended[g * rows : (g + 1) * rows] for g in range(G)], axis=1)
    part = dot_nn(flat.astype(BF), w_ref[...])
    for copy in range(8):
        out_ref[copy] = part


def attend(state, out_weight):
    return pl.pallas_call(
        attend_kernel,
        out_shape=pltpu.VMEM((8, STEPS * REQ, HD), F32),
        name="attend",
    )(pltpu.with_memory_space_constraint(state, pltpu.VMEM), out_weight)


def body(
    raw_keys,
    raw_values,
    phase,
    ratio,
    resident_len,
    beacon_queries,
    beacon_wk,
    beacon_wv,
    resident_keys,
    resident_values,
    decode_queries,
    out_weight,
):
    shard = lax.axis_index(SEQ)
    count = lax.axis_size(SEQ)
    raw_k, raw_v = raw_keys[:, :, 0], raw_values[:, :, 0]
    staged, tails = stage(beacon_wk, beacon_wv, raw_k, raw_v)
    near = lax.ppermute(tails, SEQ, [(i, i + 1) for i in range(count - 1)])
    column = lax.all_to_all(staged, "y", 0, 0).reshape(8 * HD, 2 * HD)
    weights = lax.all_gather(column, "z", axis=0, tiled=True)
    at = jnp.stack([shard, lax.axis_index("c"), (shard == count - 1).astype(jnp.int32)])
    queries = jnp.transpose(beacon_queries[:, :, 0], (0, 2, 1, 3))
    pooled = pool(at, phase, ratio, queries, raw_k, raw_v, near)
    p_own = lax.all_to_all(pooled, "x", 0, 0)
    p_other = lax.ppermute(p_own, "c", [(0, 1), (1, 0)])
    step_queries = jnp.transpose(decode_queries[:, :, 0], (2, 0, 1, 3)).reshape(ROWS, HD)
    beacon_k, beacon_v, state = project_decode(
        at,
        phase,
        ratio,
        resident_len,
        p_own,
        p_other,
        weights,
        step_queries,
        resident_keys[:, :, 0],
        resident_values[:, :, 0],
        raw_k,
        raw_v,
    )
    state = combine(lax.all_to_all(state, "y", 0, 0))
    parts = attend(lax.all_to_all(state, "z", 0, 0), out_weight)
    parts = lax.all_to_all(parts, ("x", "c"), 0, 0)
    projected = jnp.sum(parts, axis=0).astype(BF).reshape(STEPS, REQ, HD)
    return beacon_k[:, :, None], beacon_v[:, :, None], projected


def solution(mesh):
    fine = Mesh(mesh.devices.reshape(8, 8, 4, 2), ("z", "y", "x", "c"))
    head = ("x", "c")
    return jax.shard_map(
        body,
        mesh=fine,
        in_specs=(
            P(None, SEQ, head, None),
            P(None, SEQ, head, None),
            P(),
            P(),
            P(),
            P(None, SEQ, head, None, None),
            P(SEQ, head),
            P(SEQ, head),
            P(None, SEQ, head, None),
            P(None, SEQ, head, None),
            P(None, None, head, None, None),
            P(head, SEQ),
        ),
        out_specs=(
            P(None, SEQ, head, None),
            P(None, SEQ, head, None),
            P(None, None, SEQ),
        ),
        check_vma=False,
    )
```

```python
import math

import jax
import jax.numpy as jnp
from jax import lax
from jax.experimental import pallas as pl
from jax.experimental.pallas import tpu as pltpu
from jax.sharding import Mesh, PartitionSpec as P

G = 8
HD = 128
INTERVAL = 1024
NB = 128
OFF = 256
STEPS = 4
REQ = 2
RES = 256
ROWS = STEPS * REQ * G
SCALE = math.log2(math.e) / math.sqrt(HD)
MASKED = -1e30
SEQ = ("z", "y")
BF = jnp.bfloat16
F32 = jnp.float32


def dot_nt(a, b):
    return lax.dot_general(a, b, (((1,), (1,)), ((), ())), preferred_element_type=F32)


def dot_nn(a, b):
    return jnp.dot(a, b, preferred_element_type=F32)


def stage_kernel(wk_ref, wv_ref, out_ref):
    for copy in range(8):
        out_ref[copy, :, :HD] = wk_ref[...]
        out_ref[copy, :, HD:] = wv_ref[...]


def stage(wk, wv):
    return pl.pallas_call(
        stage_kernel, out_shape=pltpu.VMEM((8, HD, 2 * HD), BF), name="stage"
    )(wk, wv)


def tail_kernel(tk_ref, tv_ref, out_ref):
    out_ref[0] = tk_ref[...]
    out_ref[1] = tv_ref[...]


def tail(raw_k, raw_v):
    window = pl.BlockSpec((REQ, OFF, HD), lambda i: (0, INTERVAL // OFF - 1, 0))
    return pl.pallas_call(
        tail_kernel,
        out_shape=pltpu.VMEM((2, REQ, OFF, HD), BF),
        grid=(1,),
        in_specs=[window, window],
        out_specs=pl.BlockSpec((2, REQ, OFF, HD), lambda i: (0, 0, 0, 0)),
        name="tail",
    )(raw_k, raw_v)


def pool_kernel(at_ref, phase_ref, ratio_ref, q_ref, rk_ref, rv_ref, near_ref, out_ref):
    r = pl.program_id(0)
    shard = at_ref[0]
    phase, step = phase_ref[r], ratio_ref[r, shard]
    start = OFF - phase
    low = start + jnp.where(shard == 0, phase, 0)
    col = lax.broadcasted_iota(jnp.int32, (2 * NB, OFF + INTERVAL), 1)
    slot = lax.broadcasted_iota(jnp.int32, (2 * NB, OFF + INTERVAL), 0) % NB
    bound = jnp.minimum(low + (slot + 1) * step, start + INTERVAL)
    allowed = (col >= low) & (col < bound)
    for pair in range(G // 2):
        q = q_ref[0, 2 * pair : 2 * pair + 2].reshape(2 * NB, HD)
        scores = jnp.concatenate([dot_nt(q, near_ref[0, 0]), dot_nt(q, rk_ref[0])], axis=1)
        scores = jnp.where(allowed, scores * SCALE, MASKED)
        peak = jnp.max(scores, axis=1, keepdims=True)
        weights = jnp.exp2(scores - peak)
        total = jnp.sum(weights, axis=1, keepdims=True)
        weights = weights.astype(BF)
        weighted = dot_nn(weights[:, :OFF], near_ref[1, 0]) + dot_nn(weights[:, OFF:], rv_ref[0])
        pooled = (weighted / total).astype(BF)
        for copy in range(4):
            for half in range(2):
                at = (2 * pair + half) * HD
                out_ref[copy, :, at : at + HD] = pooled[half * NB : (half + 1) * NB]


def pool(at, phase, ratio, queries, raw_k, raw_v, near):
    return pl.pallas_call(
        pool_kernel,
        out_shape=jax.ShapeDtypeStruct((4, REQ * NB, G * HD), BF),
        grid_spec=pltpu.PrefetchScalarGridSpec(
            num_scalar_prefetch=3,
            grid=(REQ,),
            in_specs=[
                pl.BlockSpec((1, G, NB, HD), lambda r, *_: (r, 0, 0, 0)),
                pl.BlockSpec((1, INTERVAL, HD), lambda r, *_: (r, 0, 0)),
                pl.BlockSpec((1, INTERVAL, HD), lambda r, *_: (r, 0, 0)),
                pl.BlockSpec((2, 1, OFF, HD), lambda r, *_: (0, r, 0, 0)),
            ],
            out_specs=pl.BlockSpec((4, NB, G * HD), lambda r, *_: (0, r, 0)),
        ),
        compiler_params=pltpu.CompilerParams(vmem_limit_bytes=40 << 20),
        name="pool",
    )(at, phase, ratio, queries, raw_k, raw_v, near)


def pieces(value):
    high = value.astype(BF).astype(F32)
    rest = value - high
    middle = rest.astype(BF).astype(F32)
    return high, middle, rest - middle


def pack(out_ref, weighted, peak, total):
    row = lax.broadcasted_iota(jnp.int32, (16, HD), 0)
    extra = jnp.zeros((16, HD), F32)
    for at, piece in enumerate(pieces(peak) + pieces(total)):
        extra = jnp.where(row == at, piece, extra)
    weighted, extra = weighted.astype(BF), extra.astype(BF)
    for copy in range(out_ref.shape[0]):
        out_ref[copy, :ROWS] = weighted
        out_ref[copy, ROWS:] = extra


def merge(in_ref, divide):
    extra = in_ref[:, ROWS:, :].astype(F32)
    peaks = extra[:, 0] + extra[:, 1] + extra[:, 2]
    totals = extra[:, 3] + extra[:, 4] + extra[:, 5]
    peak = jnp.max(peaks, axis=0, keepdims=True)
    factors = jnp.exp2(peaks - peak)
    total = jnp.sum(totals * factors, axis=0, keepdims=True)
    scales = (factors / total if divide else factors).T
    weighted = 0.0
    for i in range(in_ref.shape[0]):
        weighted += in_ref[i, :ROWS].astype(F32) * scales[:ROWS, i : i + 1]
    return weighted, peak, total


def decode_kernel(
    at_ref, phase_ref, ratio_ref, len_ref,
    po_ref, pt_ref, w_ref, q_ref, sk_ref, sv_ref, tails_ref,
    bk_ref, bv_ref, out_ref, held, other, sems, other_sems,
):
    shard, core, last = at_ref[0], at_ref[1], at_ref[2]
    copies = [
        pltpu.make_async_copy(w_ref.at[pl.ds(k * G * HD, G * HD)], held.at[k], sems.at[k])
        for k in range(8)
    ]
    other_copies = [
        pltpu.make_async_copy(pt_ref.at[x], other.at[x], other_sems.at[x]) for x in range(4)
    ]
    for x in range(4):
        copies[2 * x].start()
        copies[2 * x + 1].start()
        other_copies[x].start()
    queries = q_ref[...]
    of_row = lax.broadcasted_iota(jnp.int32, (ROWS, RES), 0) % REQ
    col = lax.broadcasted_iota(jnp.int32, (ROWS, RES), 1)
    row = lax.broadcasted_iota(jnp.int32, (NB, 2 * HD), 0)
    live = [INTERVAL // ratio_ref[r, shard] for r in range(REQ)]

    def score(keys, usable):
        return jnp.where(usable, dot_nt(queries, keys) * SCALE, MASKED)

    early, late = [], []
    for r in range(REQ):
        mine = of_row == r
        leftover = jnp.where(last == 1, OFF - phase_ref[r], OFF)
        early.append(score(sk_ref[r], mine & (col < len_ref[r, shard])))
        early.append(score(tails_ref[0, r], mine & (col >= leftover)))
    total_part = 0.0
    for x in range(4):
        copies[2 * x].wait()
        copies[2 * x + 1].wait()
        other_copies[x].wait()
        total_part += dot_nn(po_ref[x], held[2 * x + core])
        total_part += dot_nn(other[x], held[2 * x + 1 - core])
    made = []
    for r in range(REQ):
        part = total_part[r * NB : (r + 1) * NB]
        made.append(jnp.where(row < live[r], part, 0.0).astype(BF))
        bk_ref[r] = made[r][:, :HD]
        bv_ref[r] = made[r][:, HD:]
        late.append(score(made[r][:, :HD], (of_row == r)[:, :NB] & (col[:, :NB] < live[r])))
    scores = jnp.concatenate(early + late, axis=1)
    peak = jnp.max(scores, axis=1, keepdims=True)
    weights = jnp.exp2(scores - peak)
    total = jnp.sum(weights, axis=1, keepdims=True)
    weights = weights.astype(BF)
    values = [sv_ref[0], tails_ref[1, 0], sv_ref[1], tails_ref[1, 1], made[0][:, HD:], made[1][:, HD:]]
    weighted, at = 0.0, 0
    for v in values:
        weighted += dot_nn(weights[:, at : at + v.shape[0]], v)
        at += v.shape[0]
    lane = lax.broadcasted_iota(jnp.int32, (ROWS, HD), 1)
    columns = jnp.where(lane == 0, peak, total)
    rows = jnp.concatenate([columns, jnp.zeros((HD - ROWS, HD), F32)], axis=0).T
    pack(out_ref, weighted, rows[0:1], rows[1:2])


def project_decode(at, phase, ratio, length, p_own, p_other, weights, queries, res_k, res_v, tails):
    here = lambda array: pltpu.with_memory_space_constraint(array, pltpu.VMEM)
    far = lambda array: pltpu.with_memory_space_constraint(array, pltpu.HBM)
    scalar, vmem = pl.BlockSpec(memory_space=pltpu.SMEM), pl.BlockSpec(memory_space=pltpu.VMEM)
    hbm = pl.BlockSpec(memory_space=pltpu.HBM)
    return pl.pallas_call(
        decode_kernel,
        out_shape=(
            pltpu.VMEM((REQ, NB, HD), BF),
            pltpu.VMEM((REQ, NB, HD), BF),
            pltpu.VMEM((8, ROWS + 16, HD), BF),
        ),
        in_specs=[scalar] * 4 + [vmem, hbm, hbm] + [vmem] * 4,
        out_specs=(vmem, vmem, vmem),
        scratch_shapes=[
            pltpu.VMEM((8, G * HD, 2 * HD), BF),
            pltpu.VMEM((4, REQ * NB, G * HD), BF),
            pltpu.SemaphoreType.DMA((8,)),
            pltpu.SemaphoreType.DMA((4,)),
        ],
        compiler_params=pltpu.CompilerParams(vmem_limit_bytes=40 << 20),
        name="project_decode",
    )(
        at,
        phase,
        ratio,
        length,
        here(p_own),
        far(p_other),
        far(weights),
        here(queries),
        here(res_k),
        here(res_v),
        here(tails),
    )


def combine_kernel(in_ref, out_ref):
    pack(out_ref, *merge(in_ref, False))


def combine(state):
    return pl.pallas_call(
        combine_kernel, out_shape=pltpu.VMEM(state.shape, BF), name="combine"
    )(pltpu.with_memory_space_constraint(state, pltpu.VMEM))


def attend_kernel(in_ref, w_ref, out_ref):
    attended, _, _ = merge(in_ref, True)
    rows = STEPS * REQ
    flat = jnp.concatenate([attended[g * rows : (g + 1) * rows] for g in range(G)], axis=1)
    part = dot_nn(flat.astype(BF), w_ref[...])
    high = part.astype(BF)
    both = jnp.concatenate([high.astype(F32), part - high.astype(F32)], axis=0).astype(BF)
    for copy in range(8):
        out_ref[copy] = both


def attend(state, out_weight):
    return pl.pallas_call(
        attend_kernel,
        out_shape=pltpu.VMEM((8, 2 * STEPS * REQ, HD), BF),
        name="attend",
    )(
        pltpu.with_memory_space_constraint(state, pltpu.VMEM),
        pltpu.with_memory_space_constraint(out_weight, pltpu.VMEM),
    )


def total_kernel(in_ref, out_ref):
    rows = STEPS * REQ
    both = jnp.sum(in_ref[...].astype(F32), axis=0)
    out_ref[...] = (both[:rows] + both[rows:]).astype(BF)


def total(parts):
    return pl.pallas_call(
        total_kernel, out_shape=jax.ShapeDtypeStruct((STEPS * REQ, HD), BF), name="total"
    )(pltpu.with_memory_space_constraint(parts, pltpu.VMEM))


def body(
    raw_keys,
    raw_values,
    phase,
    ratio,
    resident_len,
    beacon_queries,
    beacon_wk,
    beacon_wv,
    resident_keys,
    resident_values,
    decode_queries,
    out_weight,
):
    shard = lax.axis_index(SEQ)
    count = lax.axis_size(SEQ)
    raw_k, raw_v = raw_keys[:, :, 0], raw_values[:, :, 0]
    staged = stage(beacon_wk, beacon_wv)
    tails = tail(raw_k, raw_v)
    near = lax.ppermute(tails, SEQ, [(i, i + 1) for i in range(count - 1)])
    column = lax.all_to_all(staged, "y", 0, 0).reshape(8 * HD, 2 * HD)
    weights = lax.all_gather(column, "z", axis=0, tiled=True)
    at = jnp.stack([shard, lax.axis_index("c"), (shard == count - 1).astype(jnp.int32)])
    queries = jnp.transpose(beacon_queries[:, :, 0], (0, 2, 1, 3))
    pooled = pool(at, phase, ratio, queries, raw_k, raw_v, near)
    p_own = lax.all_to_all(pooled, "x", 0, 0)
    p_other = lax.ppermute(p_own, "c", [(0, 1), (1, 0)])
    step_queries = jnp.transpose(decode_queries[:, :, 0], (2, 0, 1, 3)).reshape(ROWS, HD)
    beacon_k, beacon_v, state = project_decode(
        at,
        phase,
        ratio,
        resident_len,
        p_own,
        p_other,
        weights,
        step_queries,
        resident_keys[:, :, 0],
        resident_values[:, :, 0],
        tails,
    )
    state = combine(lax.all_to_all(state, "y", 0, 0))
    parts = attend(lax.all_to_all(state, "z", 0, 0), out_weight)
    parts = lax.all_to_all(parts, ("x", "c"), 0, 0)
    projected = total(parts).reshape(STEPS, REQ, HD)
    return beacon_k[:, :, None], beacon_v[:, :, None], projected


def solution(mesh):
    fine = Mesh(mesh.devices.reshape(8, 8, 4, 2), ("z", "y", "x", "c"))
    head = ("x", "c")
    return jax.shard_map(
        body,
        mesh=fine,
        in_specs=(
            P(None, SEQ, head, None),
            P(None, SEQ, head, None),
            P(),
            P(),
            P(),
            P(None, SEQ, head, None, None),
            P(SEQ, head),
            P(SEQ, head),
            P(None, SEQ, head, None),
            P(None, SEQ, head, None),
            P(None, None, head, None, None),
            P(head, SEQ),
        ),
        out_specs=(
            P(None, SEQ, head, None),
            P(None, SEQ, head, None),
            P(None, None, SEQ),
        ),
        check_vma=False,
    )
```

```python
import math

import jax
import jax.numpy as jnp
from jax import lax
from jax.experimental import pallas as pl
from jax.experimental.pallas import tpu as pltpu
from jax.sharding import Mesh, PartitionSpec as P

G = 8
HD = 128
INTERVAL = 1024
NB = 128
OFF = 256
STEPS = 4
REQ = 2
RES = 256
ROWS = STEPS * REQ * G
SCALE = math.log2(math.e) / math.sqrt(HD)
MASKED = -1e30
SEQ = ("z", "y")
ALL = ("z", "y", "x", "c")
BF = jnp.bfloat16
F32 = jnp.float32


def dot_nt(a, b):
    return lax.dot_general(a, b, (((1,), (1,)), ((), ())), preferred_element_type=F32)


def dot_nn(a, b):
    return jnp.dot(a, b, preferred_element_type=F32)


def stage_kernel(wk_ref, wv_ref, out_ref):
    for copy in range(8):
        out_ref[copy, :, :HD] = wk_ref[...]
        out_ref[copy, :, HD:] = wv_ref[...]


def stage(wk, wv):
    return pl.pallas_call(
        stage_kernel, out_shape=pltpu.VMEM((8, HD, 2 * HD), BF), name="stage"
    )(wk, wv)


def tail_kernel(tk_ref, tv_ref, out_ref):
    out_ref[0] = tk_ref[...]
    out_ref[1] = tv_ref[...]


def tail(raw_k, raw_v):
    window = pl.BlockSpec((REQ, OFF, HD), lambda i: (0, INTERVAL // OFF - 1, 0))
    return pl.pallas_call(
        tail_kernel,
        out_shape=pltpu.VMEM((2, REQ, OFF, HD), BF),
        grid=(1,),
        in_specs=[window, window],
        out_specs=pl.BlockSpec((2, REQ, OFF, HD), lambda i: (0, 0, 0, 0)),
        name="tail",
    )(raw_k, raw_v)


def pool_bounds(at_ref, phase_ref, ratio_ref, start_col, width):
    r = pl.program_id(0)
    phase, step = phase_ref[r], ratio_ref[r, at_ref[0]]
    start = OFF - phase
    low = start + jnp.where(at_ref[0] == 0, phase, 0)
    col = lax.broadcasted_iota(jnp.int32, (2 * NB, width), 1) + start_col
    slot = lax.broadcasted_iota(jnp.int32, (2 * NB, width), 0) % NB
    bound = jnp.minimum(low + (slot + 1) * step, start + INTERVAL)
    return (col >= low) & (col < bound)


def pool_rows(q, keys, allowed):
    scores = jnp.where(allowed, dot_nt(q, keys) * SCALE, MASKED)
    return scores, jnp.max(scores, axis=1, keepdims=True)


def own_kernel(at_ref, phase_ref, ratio_ref, q_ref, rk_ref, rv_ref, sum_ref, stat_ref):
    allowed = pool_bounds(at_ref, phase_ref, ratio_ref, OFF, INTERVAL)
    lane = lax.broadcasted_iota(jnp.int32, (2 * NB, HD), 1)
    for pair in range(G // 2):
        q = q_ref[0, 2 * pair : 2 * pair + 2].reshape(2 * NB, HD)
        scores, peak = pool_rows(q, rk_ref[0], allowed)
        weights = jnp.exp2(scores - peak)
        total = jnp.sum(weights, axis=1, keepdims=True)
        rows = slice(2 * pair * NB, (2 * pair + 2) * NB)
        sum_ref[0, rows] = dot_nn(weights.astype(BF), rv_ref[0])
        stat_ref[0, rows] = jnp.where(lane == 0, peak, total)


def rest_kernel(at_ref, phase_ref, ratio_ref, q_ref, near_ref, sum_ref, stat_ref, out_ref):
    allowed = pool_bounds(at_ref, phase_ref, ratio_ref, 0, OFF)
    for pair in range(G // 2):
        q = q_ref[0, 2 * pair : 2 * pair + 2].reshape(2 * NB, HD)
        scores, near_peak = pool_rows(q, near_ref[0, 0], allowed)
        rows = slice(2 * pair * NB, (2 * pair + 2) * NB)
        own_peak, own_total = stat_ref[0, rows, 0:1], stat_ref[0, rows, 1:2]
        peak = jnp.maximum(near_peak, own_peak)
        weights = jnp.exp2(scores - peak)
        factor = jnp.exp2(own_peak - peak)
        total = jnp.sum(weights, axis=1, keepdims=True) + own_total * factor
        weighted = dot_nn(weights.astype(BF), near_ref[1, 0]) + sum_ref[0, rows] * factor
        pooled = (weighted / total).astype(BF)
        for copy in range(4):
            for half in range(2):
                at = (2 * pair + half) * HD
                out_ref[copy, :, at : at + HD] = pooled[half * NB : (half + 1) * NB]


QUERIES = pl.BlockSpec((1, G, NB, HD), lambda r, *_: (r, 0, 0, 0))
STATE = pl.BlockSpec((1, G * NB, HD), lambda r, *_: (r, 0, 0))


def pool_own(at, phase, ratio, queries, raw_k, raw_v):
    rows = pl.BlockSpec((1, INTERVAL, HD), lambda r, *_: (r, 0, 0))
    return pl.pallas_call(
        own_kernel,
        out_shape=(jax.ShapeDtypeStruct((REQ, G * NB, HD), F32),) * 2,
        grid_spec=pltpu.PrefetchScalarGridSpec(
            num_scalar_prefetch=3,
            grid=(REQ,),
            in_specs=[QUERIES, rows, rows],
            out_specs=(STATE, STATE),
        ),
        compiler_params=pltpu.CompilerParams(vmem_limit_bytes=24 << 20),
        name="pool_own",
    )(at, phase, ratio, queries, raw_k, raw_v)


def pool_rest(at, phase, ratio, queries, near, sums, stats):
    return pl.pallas_call(
        rest_kernel,
        out_shape=jax.ShapeDtypeStruct((4, REQ * NB, G * HD), BF),
        grid_spec=pltpu.PrefetchScalarGridSpec(
            num_scalar_prefetch=3,
            grid=(REQ,),
            in_specs=[
                QUERIES,
                pl.BlockSpec((2, 1, OFF, HD), lambda r, *_: (0, r, 0, 0)),
                STATE,
                STATE,
            ],
            out_specs=pl.BlockSpec((4, NB, G * HD), lambda r, *_: (0, r, 0)),
        ),
        compiler_params=pltpu.CompilerParams(vmem_limit_bytes=24 << 20),
        name="pool_rest",
    )(at, phase, ratio, queries, near, sums, stats)


def pieces(value):
    high = value.astype(BF).astype(F32)
    rest = value - high
    middle = rest.astype(BF).astype(F32)
    return high, middle, rest - middle


def pack(out_ref, weighted, peak, total):
    row = lax.broadcasted_iota(jnp.int32, (16, HD), 0)
    extra = jnp.zeros((16, HD), F32)
    for at, piece in enumerate(pieces(peak) + pieces(total)):
        extra = jnp.where(row == at, piece, extra)
    weighted, extra = weighted.astype(BF), extra.astype(BF)
    for copy in range(out_ref.shape[0]):
        out_ref[copy, :ROWS] = weighted
        out_ref[copy, ROWS:] = extra


def merge(in_ref, divide):
    extra = in_ref[:, ROWS:, :].astype(F32)
    peaks = extra[:, 0] + extra[:, 1] + extra[:, 2]
    totals = extra[:, 3] + extra[:, 4] + extra[:, 5]
    peak = jnp.max(peaks, axis=0, keepdims=True)
    factors = jnp.exp2(peaks - peak)
    total = jnp.sum(totals * factors, axis=0, keepdims=True)
    scales = (factors / total if divide else factors).T
    weighted = 0.0
    for i in range(in_ref.shape[0]):
        weighted += in_ref[i, :ROWS].astype(F32) * scales[:ROWS, i : i + 1]
    return weighted, peak, total


def decode_kernel(
    at_ref, phase_ref, ratio_ref, len_ref,
    po_ref, pt_ref, w_ref, q_ref, sk_ref, sv_ref, tails_ref,
    bk_ref, bv_ref, out_ref, held, other, sems, other_sems,
):
    shard, core, last = at_ref[0], at_ref[1], at_ref[2]
    copies = [pltpu.make_async_copy(w_ref.at[k], held.at[k], sems.at[k]) for k in range(8)]
    turned = [pltpu.make_async_copy(w_ref.at[:, k], held.at[k], sems.at[k]) for k in range(8)]
    other_copies = [
        pltpu.make_async_copy(pt_ref.at[x], other.at[x], other_sems.at[x]) for x in range(4)
    ]

    @pl.when(core == 0)
    def _():
        for copy in copies:
            copy.start()

    @pl.when(core != 0)
    def _():
        for copy in turned:
            copy.start()

    for copy in other_copies:
        copy.start()
    queries = q_ref[...]
    of_row = lax.broadcasted_iota(jnp.int32, (ROWS, RES), 0) % REQ
    col = lax.broadcasted_iota(jnp.int32, (ROWS, RES), 1)
    row = lax.broadcasted_iota(jnp.int32, (NB, 2 * HD), 0)
    live = [INTERVAL // ratio_ref[r, shard] for r in range(REQ)]

    def score(keys, usable):
        return jnp.where(usable, dot_nt(queries, keys) * SCALE, MASKED)

    early, late = [], []
    for r in range(REQ):
        mine = of_row == r
        leftover = jnp.where(last == 1, OFF - phase_ref[r], OFF)
        early.append(score(sk_ref[r], mine & (col < len_ref[r, shard])))
        early.append(score(tails_ref[0, r], mine & (col >= leftover)))
    total_part = 0.0
    for x in range(4):
        copies[2 * x].wait()
        copies[2 * x + 1].wait()
        other_copies[x].wait()
        total_part += dot_nn(po_ref[x], held[2 * x + core].reshape(G * HD, 2 * HD))
        total_part += dot_nn(other[x], held[2 * x + 1 - core].reshape(G * HD, 2 * HD))
    made = []
    for r in range(REQ):
        part = total_part[r * NB : (r + 1) * NB]
        made.append(jnp.where(row < live[r], part, 0.0).astype(BF))
        bk_ref[r] = made[r][:, :HD]
        bv_ref[r] = made[r][:, HD:]
        late.append(score(made[r][:, :HD], (of_row == r)[:, :NB] & (col[:, :NB] < live[r])))
    scores = jnp.concatenate(early + late, axis=1)
    peak = jnp.max(scores, axis=1, keepdims=True)
    weights = jnp.exp2(scores - peak)
    total = jnp.sum(weights, axis=1, keepdims=True)
    weights = weights.astype(BF)
    values = [sv_ref[0], tails_ref[1, 0], sv_ref[1], tails_ref[1, 1], made[0][:, HD:], made[1][:, HD:]]
    weighted, at = 0.0, 0
    for v in values:
        weighted += dot_nn(weights[:, at : at + v.shape[0]], v)
        at += v.shape[0]
    lane = lax.broadcasted_iota(jnp.int32, (ROWS, HD), 1)
    columns = jnp.where(lane == 0, peak, total)
    rows = jnp.concatenate([columns, jnp.zeros((HD - ROWS, HD), F32)], axis=0).T
    pack(out_ref, weighted, rows[0:1], rows[1:2])


def project_decode(at, phase, ratio, length, p_own, p_other, weights, queries, res_k, res_v, tails):
    here = lambda array: pltpu.with_memory_space_constraint(array, pltpu.VMEM)
    far = lambda array: pltpu.with_memory_space_constraint(array, pltpu.HBM)
    scalar, vmem = pl.BlockSpec(memory_space=pltpu.SMEM), pl.BlockSpec(memory_space=pltpu.VMEM)
    hbm = pl.BlockSpec(memory_space=pltpu.HBM)
    return pl.pallas_call(
        decode_kernel,
        out_shape=(
            pltpu.VMEM((REQ, NB, HD), BF),
            pltpu.VMEM((REQ, NB, HD), BF),
            pltpu.VMEM((8, ROWS + 16, HD), BF),
        ),
        in_specs=[scalar] * 4 + [vmem, hbm, hbm] + [vmem] * 4,
        out_specs=(vmem, vmem, vmem),
        scratch_shapes=[
            pltpu.VMEM((8, 8, HD, 2 * HD), BF),
            pltpu.VMEM((4, REQ * NB, G * HD), BF),
            pltpu.SemaphoreType.DMA((8,)),
            pltpu.SemaphoreType.DMA((4,)),
        ],
        compiler_params=pltpu.CompilerParams(vmem_limit_bytes=40 << 20),
        name="project_decode",
    )(
        at,
        phase,
        ratio,
        length,
        here(p_own),
        far(p_other),
        far(weights),
        here(queries),
        here(res_k),
        here(res_v),
        here(tails),
    )


def combine_kernel(in_ref, out_ref):
    pack(out_ref, *merge(in_ref, False))


def combine(state):
    return pl.pallas_call(
        combine_kernel, out_shape=pltpu.VMEM(state.shape, BF), name="combine"
    )(pltpu.with_memory_space_constraint(state, pltpu.VMEM))


def attend_kernel(in_ref, w_ref, out_ref):
    attended, _, _ = merge(in_ref, True)
    rows = STEPS * REQ
    flat = jnp.concatenate([attended[g * rows : (g + 1) * rows] for g in range(G)], axis=1)
    part = dot_nn(flat.astype(BF), w_ref[...])
    high = part.astype(BF)
    both = jnp.concatenate([high.astype(F32), part - high.astype(F32)], axis=0).astype(BF)
    for copy in range(8):
        out_ref[copy] = both


def attend(state, out_weight):
    return pl.pallas_call(
        attend_kernel,
        out_shape=pltpu.VMEM((8, 2 * STEPS * REQ, HD), BF),
        name="attend",
    )(
        pltpu.with_memory_space_constraint(state, pltpu.VMEM),
        pltpu.with_memory_space_constraint(out_weight, pltpu.VMEM),
    )


def total_kernel(in_ref, out_ref):
    rows = STEPS * REQ
    both = jnp.sum(in_ref[...].astype(F32), axis=0)
    out_ref[...] = (both[:rows] + both[rows:]).astype(BF)


def total(parts):
    return pl.pallas_call(
        total_kernel, out_shape=jax.ShapeDtypeStruct((STEPS * REQ, HD), BF), name="total"
    )(pltpu.with_memory_space_constraint(parts, pltpu.VMEM))


def lines(axes):
    def device(z, y, x, c):
        return ((z * 8 + y) * 4 + x) * 2 + c

    return [
        [device(i, j, x, c) if axes[c] == "z" else device(j, i, x, c) for i in range(8)]
        for c in range(2)
        for x in range(4)
        for j in range(8)
    ]


def body(
    raw_keys,
    raw_values,
    phase,
    ratio,
    resident_len,
    beacon_queries,
    beacon_wk,
    beacon_wv,
    resident_keys,
    resident_values,
    decode_queries,
    out_weight,
):
    shard = lax.axis_index(SEQ)
    count = lax.axis_size(SEQ)
    raw_k, raw_v = raw_keys[:, :, 0], raw_values[:, :, 0]
    staged = stage(beacon_wk, beacon_wv)
    tails = tail(raw_k, raw_v)
    near = lax.ppermute(tails, SEQ, [(i, i + 1) for i in range(count - 1)])
    column = lax.all_to_all(staged, ALL, 0, 0, axis_index_groups=lines("yz"))
    column = column.reshape(8 * HD, 2 * HD)
    at = jnp.stack([shard, lax.axis_index("c"), (shard == count - 1).astype(jnp.int32)])
    queries = jnp.transpose(beacon_queries[:, :, 0], (0, 2, 1, 3))
    sums, stats = pool_own(at, phase, ratio, queries, raw_k, raw_v)
    column, sums, stats = lax.optimization_barrier((column, sums, stats))
    weights = lax.all_gather(column, ALL, axis=0, tiled=True, axis_index_groups=lines("zy"))
    weights = weights.reshape(8, 8, HD, 2 * HD)
    pooled = pool_rest(at, phase, ratio, queries, near, sums, stats)
    p_own = lax.all_to_all(pooled, "x", 0, 0)
    p_other = lax.ppermute(p_own, "c", [(0, 1), (1, 0)])
    step_queries = jnp.transpose(decode_queries[:, :, 0], (2, 0, 1, 3)).reshape(ROWS, HD)
    beacon_k, beacon_v, state = project_decode(
        at,
        phase,
        ratio,
        resident_len,
        p_own,
        p_other,
        weights,
        step_queries,
        resident_keys[:, :, 0],
        resident_values[:, :, 0],
        tails,
    )
    state = combine(lax.all_to_all(state, "y", 0, 0))
    parts = attend(lax.all_to_all(state, "z", 0, 0), out_weight)
    parts = lax.all_to_all(parts, ("x", "c"), 0, 0)
    projected = total(parts).reshape(STEPS, REQ, HD)
    return beacon_k[:, :, None], beacon_v[:, :, None], projected


def solution(mesh):
    fine = Mesh(mesh.devices.reshape(8, 8, 4, 2), ("z", "y", "x", "c"))
    head = ("x", "c")
    return jax.shard_map(
        body,
        mesh=fine,
        in_specs=(
            P(None, SEQ, head, None),
            P(None, SEQ, head, None),
            P(),
            P(),
            P(),
            P(None, SEQ, head, None, None),
            P(SEQ, head),
            P(SEQ, head),
            P(None, SEQ, head, None),
            P(None, SEQ, head, None),
            P(None, None, head, None, None),
            P(head, SEQ),
        ),
        out_specs=(
            P(None, SEQ, head, None),
            P(None, SEQ, head, None),
            P(None, None, SEQ),
        ),
        check_vma=False,
    )
```

```python
import math

import jax
import jax.numpy as jnp
from jax import lax
from jax.experimental import pallas as pl
from jax.experimental.pallas import tpu as pltpu
from jax.sharding import Mesh, PartitionSpec as P

G = 8
HD = 128
INTERVAL = 1024
NB = 128
OFF = 256
STEPS = 4
REQ = 2
RES = 256
ROWS = STEPS * REQ * G
SCALE = math.log2(math.e) / math.sqrt(HD)
MASKED = -1e30
SEQ = ("z", "y")
ALL = ("z", "y", "x", "c")
BF = jnp.bfloat16
F32 = jnp.float32


def dot_nt(a, b):
    return lax.dot_general(a, b, (((1,), (1,)), ((), ())), preferred_element_type=F32)


def dot_nn(a, b):
    return jnp.dot(a, b, preferred_element_type=F32)


def stage_kernel(wk_ref, wv_ref, out_ref):
    for copy in range(8):
        out_ref[copy, :, :HD] = wk_ref[...]
        out_ref[copy, :, HD:] = wv_ref[...]


def stage(wk, wv):
    return pl.pallas_call(
        stage_kernel, out_shape=pltpu.VMEM((8, HD, 2 * HD), BF), name="stage"
    )(wk, wv)


def tail_kernel(tk_ref, tv_ref, out_ref):
    out_ref[0] = tk_ref[...]
    out_ref[1] = tv_ref[...]


def tail(raw_k, raw_v):
    window = pl.BlockSpec((REQ, OFF, HD), lambda i: (0, INTERVAL // OFF - 1, 0))
    return pl.pallas_call(
        tail_kernel,
        out_shape=pltpu.VMEM((2, REQ, OFF, HD), BF),
        grid=(1,),
        in_specs=[window, window],
        out_specs=pl.BlockSpec((2, REQ, OFF, HD), lambda i: (0, 0, 0, 0)),
        name="tail",
    )(raw_k, raw_v)


def pool_bounds(at_ref, phase_ref, ratio_ref, start_col, width):
    r = pl.program_id(0)
    phase, step = phase_ref[r], ratio_ref[r, at_ref[0]]
    start = OFF - phase
    low = start + jnp.where(at_ref[0] == 0, phase, 0)
    col = lax.broadcasted_iota(jnp.int32, (2 * NB, width), 1) + start_col
    slot = lax.broadcasted_iota(jnp.int32, (2 * NB, width), 0) % NB
    bound = jnp.minimum(low + (slot + 1) * step, start + INTERVAL)
    return (col >= low) & (col < bound)


def pool_rows(q, keys, allowed):
    scores = jnp.where(allowed, dot_nt(q, keys) * SCALE, MASKED)
    return scores, jnp.max(scores, axis=1, keepdims=True)


def own_kernel(at_ref, phase_ref, ratio_ref, q_ref, rk_ref, rv_ref, sum_ref, stat_ref):
    allowed = pool_bounds(at_ref, phase_ref, ratio_ref, OFF, INTERVAL)
    for pair in range(G // 2):
        q = q_ref[0, 2 * pair : 2 * pair + 2].reshape(2 * NB, HD)
        scores, peak = pool_rows(q, rk_ref[0], allowed)
        weights = jnp.exp2(scores - peak)
        total = jnp.sum(weights, axis=1, keepdims=True)
        rows = slice(2 * pair * NB, (2 * pair + 2) * NB)
        sum_ref[0, rows] = (dot_nn(weights.astype(BF), rv_ref[0]) / total).astype(BF)
        stat_ref[0, rows] = jnp.broadcast_to(peak + jnp.log2(total), (2 * NB, HD))


def rest_kernel(at_ref, phase_ref, ratio_ref, q_ref, near_ref, sum_ref, stat_ref, out_ref):
    allowed = pool_bounds(at_ref, phase_ref, ratio_ref, 0, OFF)
    values = jnp.concatenate([near_ref[1, 0], jnp.ones((OFF, HD), BF)], axis=1)
    for pair in range(G // 2):
        q = q_ref[0, 2 * pair : 2 * pair + 2].reshape(2 * NB, HD)
        scores, near_peak = pool_rows(q, near_ref[0, 0], allowed)
        rows = slice(2 * pair * NB, (2 * pair + 2) * NB)
        own = stat_ref[0, rows]
        peak = jnp.maximum(near_peak, own)
        weights = jnp.exp2(scores - jnp.concatenate([peak, peak], axis=1)).astype(BF)
        factor = jnp.exp2(own - peak)
        both = dot_nn(weights, values)
        total = both[:, HD:] + factor
        weighted = both[:, :HD] + sum_ref[0, rows].astype(F32) * factor
        pooled = (weighted / total).astype(BF)
        for copy in range(4):
            for half in range(2):
                at = (2 * pair + half) * HD
                out_ref[copy, :, at : at + HD] = pooled[half * NB : (half + 1) * NB]


QUERIES = pl.BlockSpec((1, G, NB, HD), lambda r, *_: (r, 0, 0, 0))
STATE = pl.BlockSpec((1, G * NB, HD), lambda r, *_: (r, 0, 0))


def pool_own(at, phase, ratio, queries, raw_k, raw_v):
    rows = pl.BlockSpec((1, INTERVAL, HD), lambda r, *_: (r, 0, 0))
    return pl.pallas_call(
        own_kernel,
        out_shape=(
            jax.ShapeDtypeStruct((REQ, G * NB, HD), BF),
            jax.ShapeDtypeStruct((REQ, G * NB, HD), F32),
        ),
        grid_spec=pltpu.PrefetchScalarGridSpec(
            num_scalar_prefetch=3,
            grid=(REQ,),
            in_specs=[QUERIES, rows, rows],
            out_specs=(STATE, STATE),
        ),
        compiler_params=pltpu.CompilerParams(vmem_limit_bytes=24 << 20),
        name="pool_own",
    )(at, phase, ratio, queries, raw_k, raw_v)


def pool_rest(at, phase, ratio, queries, near, sums, stats):
    return pl.pallas_call(
        rest_kernel,
        out_shape=jax.ShapeDtypeStruct((4, REQ * NB, G * HD), BF),
        grid_spec=pltpu.PrefetchScalarGridSpec(
            num_scalar_prefetch=3,
            grid=(REQ,),
            in_specs=[
                QUERIES,
                pl.BlockSpec((2, 1, OFF, HD), lambda r, *_: (0, r, 0, 0)),
                STATE,
                STATE,
            ],
            out_specs=pl.BlockSpec((4, NB, G * HD), lambda r, *_: (0, r, 0)),
        ),
        compiler_params=pltpu.CompilerParams(vmem_limit_bytes=24 << 20),
        name="pool_rest",
    )(at, phase, ratio, queries, near, sums, stats)


def pieces(value):
    high = value.astype(BF).astype(F32)
    rest = value - high
    middle = rest.astype(BF).astype(F32)
    return high, middle, rest - middle


def pack(out_ref, weighted, peak, total):
    row = lax.broadcasted_iota(jnp.int32, (16, HD), 0)
    extra = jnp.zeros((16, HD), F32)
    for at, piece in enumerate(pieces(peak) + pieces(total)):
        extra = jnp.where(row == at, piece, extra)
    weighted, extra = weighted.astype(BF), extra.astype(BF)
    for copy in range(out_ref.shape[0]):
        out_ref[copy, :ROWS] = weighted
        out_ref[copy, ROWS:] = extra


def merge(in_ref, divide):
    extra = in_ref[:, ROWS:, :].astype(F32)
    peaks = extra[:, 0] + extra[:, 1] + extra[:, 2]
    totals = extra[:, 3] + extra[:, 4] + extra[:, 5]
    peak = jnp.max(peaks, axis=0, keepdims=True)
    factors = jnp.exp2(peaks - peak)
    total = jnp.sum(totals * factors, axis=0, keepdims=True)
    scales = (factors / total if divide else factors).T
    weighted = 0.0
    for i in range(in_ref.shape[0]):
        weighted += in_ref[i, :ROWS].astype(F32) * scales[:ROWS, i : i + 1]
    return weighted, peak, total


def decode_kernel(
    at_ref, phase_ref, ratio_ref, len_ref,
    po_ref, pt_ref, w_ref, q_ref, sk_ref, sv_ref, tails_ref,
    bk_ref, bv_ref, out_ref, held, other, sems, other_sems,
):
    shard, core, last = at_ref[0], at_ref[1], at_ref[2]
    copies = [pltpu.make_async_copy(w_ref.at[k], held.at[k], sems.at[k]) for k in range(8)]
    turned = [pltpu.make_async_copy(w_ref.at[:, k], held.at[k], sems.at[k]) for k in range(8)]
    other_copies = [
        pltpu.make_async_copy(pt_ref.at[x], other.at[x], other_sems.at[x]) for x in range(4)
    ]

    @pl.when(core == 0)
    def _():
        for copy in copies:
            copy.start()

    @pl.when(core != 0)
    def _():
        for copy in turned:
            copy.start()

    for copy in other_copies:
        copy.start()
    queries = q_ref[...]
    of_row = lax.broadcasted_iota(jnp.int32, (ROWS, RES), 0) % REQ
    col = lax.broadcasted_iota(jnp.int32, (ROWS, RES), 1)
    row = lax.broadcasted_iota(jnp.int32, (NB, 2 * HD), 0)
    live = [INTERVAL // ratio_ref[r, shard] for r in range(REQ)]

    def score(keys, usable):
        return jnp.where(usable, dot_nt(queries, keys) * SCALE, MASKED)

    early, late = [], []
    for r in range(REQ):
        mine = of_row == r
        leftover = jnp.where(last == 1, OFF - phase_ref[r], OFF)
        early.append(score(sk_ref[r], mine & (col < len_ref[r, shard])))
        early.append(score(tails_ref[0, r], mine & (col >= leftover)))
    total_part = 0.0
    for x in range(4):
        copies[2 * x].wait()
        copies[2 * x + 1].wait()
        other_copies[x].wait()
        total_part += dot_nn(po_ref[x], held[2 * x + core].reshape(G * HD, 2 * HD))
        total_part += dot_nn(other[x], held[2 * x + 1 - core].reshape(G * HD, 2 * HD))
    made = []
    for r in range(REQ):
        part = total_part[r * NB : (r + 1) * NB]
        made.append(jnp.where(row < live[r], part, 0.0).astype(BF))
        bk_ref[r] = made[r][:, :HD]
        bv_ref[r] = made[r][:, HD:]
        late.append(score(made[r][:, :HD], (of_row == r)[:, :NB] & (col[:, :NB] < live[r])))
    scores = jnp.concatenate(early + late, axis=1)
    peak = jnp.max(scores, axis=1, keepdims=True)
    weights = jnp.exp2(scores - peak)
    total = jnp.sum(weights, axis=1, keepdims=True)
    weights = weights.astype(BF)
    values = [sv_ref[0], tails_ref[1, 0], sv_ref[1], tails_ref[1, 1], made[0][:, HD:], made[1][:, HD:]]
    weighted, at = 0.0, 0
    for v in values:
        weighted += dot_nn(weights[:, at : at + v.shape[0]], v)
        at += v.shape[0]
    lane = lax.broadcasted_iota(jnp.int32, (ROWS, HD), 1)
    columns = jnp.where(lane == 0, peak, total)
    rows = jnp.concatenate([columns, jnp.zeros((HD - ROWS, HD), F32)], axis=0).T
    pack(out_ref, weighted, rows[0:1], rows[1:2])


def project_decode(at, phase, ratio, length, p_own, p_other, weights, queries, res_k, res_v, tails):
    here = lambda array: pltpu.with_memory_space_constraint(array, pltpu.VMEM)
    far = lambda array: pltpu.with_memory_space_constraint(array, pltpu.HBM)
    scalar, vmem = pl.BlockSpec(memory_space=pltpu.SMEM), pl.BlockSpec(memory_space=pltpu.VMEM)
    hbm = pl.BlockSpec(memory_space=pltpu.HBM)
    return pl.pallas_call(
        decode_kernel,
        out_shape=(
            pltpu.VMEM((REQ, NB, HD), BF),
            pltpu.VMEM((REQ, NB, HD), BF),
            pltpu.VMEM((8, ROWS + 16, HD), BF),
        ),
        in_specs=[scalar] * 4 + [vmem, hbm, hbm] + [vmem] * 4,
        out_specs=(vmem, vmem, vmem),
        scratch_shapes=[
            pltpu.VMEM((8, 8, HD, 2 * HD), BF),
            pltpu.VMEM((4, REQ * NB, G * HD), BF),
            pltpu.SemaphoreType.DMA((8,)),
            pltpu.SemaphoreType.DMA((4,)),
        ],
        compiler_params=pltpu.CompilerParams(vmem_limit_bytes=40 << 20),
        name="project_decode",
    )(
        at,
        phase,
        ratio,
        length,
        here(p_own),
        far(p_other),
        far(weights),
        here(queries),
        here(res_k),
        here(res_v),
        here(tails),
    )


def combine_kernel(in_ref, out_ref):
    pack(out_ref, *merge(in_ref, False))


def combine(state):
    return pl.pallas_call(
        combine_kernel, out_shape=pltpu.VMEM(state.shape, BF), name="combine"
    )(pltpu.with_memory_space_constraint(state, pltpu.VMEM))


def attend_kernel(in_ref, w_ref, out_ref):
    attended, _, _ = merge(in_ref, True)
    rows = STEPS * REQ
    flat = jnp.concatenate([attended[g * rows : (g + 1) * rows] for g in range(G)], axis=1)
    part = dot_nn(flat.astype(BF), w_ref[...])
    high = part.astype(BF)
    both = jnp.concatenate([high.astype(F32), part - high.astype(F32)], axis=0).astype(BF)
    for copy in range(8):
        out_ref[copy] = both


def attend(state, out_weight):
    return pl.pallas_call(
        attend_kernel,
        out_shape=pltpu.VMEM((8, 2 * STEPS * REQ, HD), BF),
        name="attend",
    )(
        pltpu.with_memory_space_constraint(state, pltpu.VMEM),
        pltpu.with_memory_space_constraint(out_weight, pltpu.VMEM),
    )


def total_kernel(in_ref, out_ref):
    rows = STEPS * REQ
    both = jnp.sum(in_ref[...].astype(F32), axis=0)
    out_ref[...] = (both[:rows] + both[rows:]).astype(BF)


def total(parts):
    return pl.pallas_call(
        total_kernel, out_shape=jax.ShapeDtypeStruct((STEPS * REQ, HD), BF), name="total"
    )(pltpu.with_memory_space_constraint(parts, pltpu.VMEM))


def lines(axes):
    def device(z, y, x, c):
        return ((z * 8 + y) * 4 + x) * 2 + c

    return [
        [device(i, j, x, c) if axes[c] == "z" else device(j, i, x, c) for i in range(8)]
        for c in range(2)
        for x in range(4)
        for j in range(8)
    ]


def body(
    raw_keys,
    raw_values,
    phase,
    ratio,
    resident_len,
    beacon_queries,
    beacon_wk,
    beacon_wv,
    resident_keys,
    resident_values,
    decode_queries,
    out_weight,
):
    shard = lax.axis_index(SEQ)
    count = lax.axis_size(SEQ)
    raw_k, raw_v = raw_keys[:, :, 0], raw_values[:, :, 0]
    staged = stage(beacon_wk, beacon_wv)
    tails = tail(raw_k, raw_v)
    column = lax.all_to_all(staged, ALL, 0, 0, axis_index_groups=lines("yz"))
    column = column.reshape(8 * HD, 2 * HD)
    at = jnp.stack([shard, lax.axis_index("c"), (shard == count - 1).astype(jnp.int32)])
    queries = jnp.transpose(beacon_queries[:, :, 0], (0, 2, 1, 3))
    sums, stats = pool_own(at, phase, ratio, queries, raw_k, raw_v)
    column, sums, stats, tails = lax.optimization_barrier((column, sums, stats, tails))
    near = lax.ppermute(tails, SEQ, [(i, i + 1) for i in range(count - 1)])
    weights = lax.all_gather(column, ALL, axis=0, tiled=True, axis_index_groups=lines("zy"))
    weights = weights.reshape(8, 8, HD, 2 * HD)
    pooled = pool_rest(at, phase, ratio, queries, near, sums, stats)
    p_own = lax.all_to_all(pooled, "x", 0, 0)
    p_other = lax.ppermute(p_own, "c", [(0, 1), (1, 0)])
    step_queries = jnp.transpose(decode_queries[:, :, 0], (2, 0, 1, 3)).reshape(ROWS, HD)
    beacon_k, beacon_v, state = project_decode(
        at,
        phase,
        ratio,
        resident_len,
        p_own,
        p_other,
        weights,
        step_queries,
        resident_keys[:, :, 0],
        resident_values[:, :, 0],
        tails,
    )
    state = combine(lax.all_to_all(state, "y", 0, 0))
    parts = attend(lax.all_to_all(state, "z", 0, 0), out_weight)
    parts = lax.all_to_all(parts, ("x", "c"), 0, 0)
    projected = total(parts).reshape(STEPS, REQ, HD)
    return beacon_k[:, :, None], beacon_v[:, :, None], projected


def solution(mesh):
    fine = Mesh(mesh.devices.reshape(8, 8, 4, 2), ("z", "y", "x", "c"))
    head = ("x", "c")
    return jax.shard_map(
        body,
        mesh=fine,
        in_specs=(
            P(None, SEQ, head, None),
            P(None, SEQ, head, None),
            P(),
            P(),
            P(),
            P(None, SEQ, head, None, None),
            P(SEQ, head),
            P(SEQ, head),
            P(None, SEQ, head, None),
            P(None, SEQ, head, None),
            P(None, None, head, None, None),
            P(head, SEQ),
        ),
        out_specs=(
            P(None, SEQ, head, None),
            P(None, SEQ, head, None),
            P(None, None, SEQ),
        ),
        check_vma=False,
    )
```

```python
import math

import jax
import jax.numpy as jnp
from jax import lax
from jax.experimental import pallas as pl
from jax.experimental.pallas import tpu as pltpu
from jax.sharding import Mesh, PartitionSpec as P

G = 8
HD = 128
INTERVAL = 1024
NB = 128
OFF = 256
STEPS = 4
REQ = 2
RES = 256
ROWS = STEPS * REQ * G
SCALE = math.log2(math.e) / math.sqrt(HD)
MASKED = -1e30
SEQ = ("z", "y")
ALL = ("z", "y", "x", "c")
BF = jnp.bfloat16
F32 = jnp.float32


def dot_nt(a, b):
    return lax.dot_general(a, b, (((1,), (1,)), ((), ())), preferred_element_type=F32)


def dot_nn(a, b):
    return jnp.dot(a, b, preferred_element_type=F32)


def stage_kernel(wk_ref, wv_ref, out_ref):
    for copy in range(8):
        out_ref[copy, :, :HD] = wk_ref[...]
        out_ref[copy, :, HD:] = wv_ref[...]


def stage(wk, wv):
    return pl.pallas_call(
        stage_kernel, out_shape=pltpu.VMEM((8, HD, 2 * HD), BF), name="stage"
    )(wk, wv)


def tail_kernel(tk_ref, tv_ref, out_ref):
    out_ref[0] = tk_ref[...]
    out_ref[1] = tv_ref[...]


def tail(raw_k, raw_v):
    window = pl.BlockSpec((REQ, OFF, HD), lambda i: (0, INTERVAL // OFF - 1, 0))
    return pl.pallas_call(
        tail_kernel,
        out_shape=pltpu.VMEM((2, REQ, OFF, HD), BF),
        grid=(1,),
        in_specs=[window, window],
        out_specs=pl.BlockSpec((2, REQ, OFF, HD), lambda i: (0, 0, 0, 0)),
        name="tail",
    )(raw_k, raw_v)


def pool_bounds(at_ref, phase_ref, ratio_ref, start_col, width):
    r = pl.program_id(0)
    phase, step = phase_ref[r], ratio_ref[r, at_ref[0]]
    start = OFF - phase
    low = start + jnp.where(at_ref[0] == 0, phase, 0)
    col = lax.broadcasted_iota(jnp.int32, (2 * NB, width), 1) + start_col
    slot = lax.broadcasted_iota(jnp.int32, (2 * NB, width), 0) % NB
    bound = jnp.minimum(low + (slot + 1) * step, start + INTERVAL)
    return (col >= low) & (col < bound)


def pool_rows(q, keys, allowed):
    scores = jnp.where(allowed, dot_nt(q, keys) * SCALE, MASKED)
    return scores, jnp.max(scores, axis=1, keepdims=True)


def own_kernel(at_ref, phase_ref, ratio_ref, q_ref, rk_ref, rv_ref, sum_ref, stat_ref):
    allowed = pool_bounds(at_ref, phase_ref, ratio_ref, OFF, INTERVAL)
    for pair in range(G // 2):
        q = q_ref[0, 2 * pair : 2 * pair + 2].reshape(2 * NB, HD)
        scores, peak = pool_rows(q, rk_ref[0], allowed)
        weights = jnp.exp2(scores - peak)
        total = jnp.sum(weights, axis=1, keepdims=True)
        rows = slice(2 * pair * NB, (2 * pair + 2) * NB)
        sum_ref[0, rows] = (dot_nn(weights.astype(BF), rv_ref[0]) / total).astype(BF)
        stat_ref[0, rows] = jnp.broadcast_to(peak + jnp.log2(total), (2 * NB, HD))


def rest_kernel(at_ref, phase_ref, ratio_ref, q_ref, near_ref, sum_ref, stat_ref, out_ref):
    allowed = pool_bounds(at_ref, phase_ref, ratio_ref, 0, OFF)
    values = jnp.concatenate([near_ref[1, 0], jnp.ones((OFF, HD), BF)], axis=1)
    for pair in range(G // 2):
        q = q_ref[0, 2 * pair : 2 * pair + 2].reshape(2 * NB, HD)
        scores, near_peak = pool_rows(q, near_ref[0, 0], allowed)
        rows = slice(2 * pair * NB, (2 * pair + 2) * NB)
        own = stat_ref[0, rows]
        peak = jnp.maximum(near_peak, own)
        weights = jnp.exp2(scores - jnp.concatenate([peak, peak], axis=1)).astype(BF)
        factor = jnp.exp2(own - peak)
        both = dot_nn(weights, values)
        total = both[:, HD:] + factor
        weighted = both[:, :HD] + sum_ref[0, rows].astype(F32) * factor
        pooled = (weighted / total).astype(BF)
        for copy in range(4):
            for half in range(2):
                at = (2 * pair + half) * HD
                out_ref[copy, :, at : at + HD] = pooled[half * NB : (half + 1) * NB]


QUERIES = pl.BlockSpec((1, G, NB, HD), lambda r, *_: (r, 0, 0, 0))
STATE = pl.BlockSpec((1, G * NB, HD), lambda r, *_: (r, 0, 0))


def pool_own(at, phase, ratio, queries, raw_k, raw_v):
    rows = pl.BlockSpec((1, INTERVAL, HD), lambda r, *_: (r, 0, 0))
    return pl.pallas_call(
        own_kernel,
        out_shape=(
            jax.ShapeDtypeStruct((REQ, G * NB, HD), BF),
            jax.ShapeDtypeStruct((REQ, G * NB, HD), F32),
        ),
        grid_spec=pltpu.PrefetchScalarGridSpec(
            num_scalar_prefetch=3,
            grid=(REQ,),
            in_specs=[QUERIES, rows, rows],
            out_specs=(STATE, STATE),
        ),
        compiler_params=pltpu.CompilerParams(vmem_limit_bytes=24 << 20),
        name="pool_own",
    )(at, phase, ratio, queries, raw_k, raw_v)


def pool_rest(at, phase, ratio, queries, near, sums, stats):
    return pl.pallas_call(
        rest_kernel,
        out_shape=jax.ShapeDtypeStruct((4, REQ * NB, G * HD), BF),
        grid_spec=pltpu.PrefetchScalarGridSpec(
            num_scalar_prefetch=3,
            grid=(REQ,),
            in_specs=[
                QUERIES,
                pl.BlockSpec((2, 1, OFF, HD), lambda r, *_: (0, r, 0, 0)),
                STATE,
                STATE,
            ],
            out_specs=pl.BlockSpec((4, NB, G * HD), lambda r, *_: (0, r, 0)),
        ),
        compiler_params=pltpu.CompilerParams(vmem_limit_bytes=24 << 20),
        name="pool_rest",
    )(at, phase, ratio, queries, near, sums, stats)


def pieces(value):
    high = value.astype(BF).astype(F32)
    rest = value - high
    middle = rest.astype(BF).astype(F32)
    return high, middle, rest - middle


def pack(out_ref, weighted, peak, total):
    row = lax.broadcasted_iota(jnp.int32, (16, HD), 0)
    extra = jnp.zeros((16, HD), F32)
    for at, piece in enumerate(pieces(peak) + pieces(total)):
        extra = jnp.where(row == at, piece, extra)
    weighted, extra = weighted.astype(BF), extra.astype(BF)
    for copy in range(out_ref.shape[0]):
        out_ref[copy, :ROWS] = weighted
        out_ref[copy, ROWS:] = extra


def merge(in_ref, divide):
    extra = in_ref[:, ROWS:, :].astype(F32)
    peaks = extra[:, 0] + extra[:, 1] + extra[:, 2]
    totals = extra[:, 3] + extra[:, 4] + extra[:, 5]
    peak = jnp.max(peaks, axis=0, keepdims=True)
    factors = jnp.exp2(peaks - peak)
    total = jnp.sum(totals * factors, axis=0, keepdims=True)
    scales = (factors / total if divide else factors).T
    weighted = 0.0
    for i in range(in_ref.shape[0]):
        weighted += in_ref[i, :ROWS].astype(F32) * scales[:ROWS, i : i + 1]
    return weighted, peak, total


def decode_kernel(
    at_ref, phase_ref, ratio_ref, len_ref,
    po_ref, pt_ref, w_ref, q_ref, sk_ref, sv_ref, tails_ref,
    bk_ref, bv_ref, out_ref, held, other, sems, other_sems,
):
    shard, core, last = at_ref[0], at_ref[1], at_ref[2]
    copies = [pltpu.make_async_copy(w_ref.at[k], held.at[k], sems.at[k]) for k in range(8)]
    turned = [pltpu.make_async_copy(w_ref.at[:, k], held.at[k], sems.at[k]) for k in range(8)]
    other_copies = [
        pltpu.make_async_copy(pt_ref.at[x], other.at[x], other_sems.at[x]) for x in range(4)
    ]

    @pl.when(core == 0)
    def _():
        for copy in copies:
            copy.start()

    @pl.when(core != 0)
    def _():
        for copy in turned:
            copy.start()

    for copy in other_copies:
        copy.start()
    queries = q_ref[...]
    of_row = lax.broadcasted_iota(jnp.int32, (ROWS, RES), 0) % REQ
    col = lax.broadcasted_iota(jnp.int32, (ROWS, RES), 1)
    row = lax.broadcasted_iota(jnp.int32, (NB, 2 * HD), 0)
    live = [INTERVAL // ratio_ref[r, shard] for r in range(REQ)]

    def score(keys, usable):
        return jnp.where(usable, dot_nt(queries, keys) * SCALE, MASKED)

    early, late = [], []
    for r in range(REQ):
        mine = of_row == r
        leftover = jnp.where(last == 1, OFF - phase_ref[r], OFF)
        early.append(score(sk_ref[r], mine & (col < len_ref[r, shard])))
        early.append(score(tails_ref[0, r], mine & (col >= leftover)))
    total_part = 0.0
    for x in range(4):
        copies[2 * x].wait()
        copies[2 * x + 1].wait()
        other_copies[x].wait()
        total_part += dot_nn(po_ref[x], held[2 * x + core].reshape(G * HD, 2 * HD))
        total_part += dot_nn(other[x], held[2 * x + 1 - core].reshape(G * HD, 2 * HD))
    made = []
    for r in range(REQ):
        part = total_part[r * NB : (r + 1) * NB]
        made.append(jnp.where(row < live[r], part, 0.0).astype(BF))
        bk_ref[r] = made[r][:, :HD]
        bv_ref[r] = made[r][:, HD:]
        late.append(score(made[r][:, :HD], (of_row == r)[:, :NB] & (col[:, :NB] < live[r])))
    scores = jnp.concatenate(early + late, axis=1)
    peak = jnp.max(scores, axis=1, keepdims=True)
    weights = jnp.exp2(scores - peak)
    total = jnp.sum(weights, axis=1, keepdims=True)
    weights = weights.astype(BF)
    values = [sv_ref[0], tails_ref[1, 0], sv_ref[1], tails_ref[1, 1], made[0][:, HD:], made[1][:, HD:]]
    weighted, at = 0.0, 0
    for v in values:
        weighted += dot_nn(weights[:, at : at + v.shape[0]], v)
        at += v.shape[0]
    lane = lax.broadcasted_iota(jnp.int32, (ROWS, HD), 1)
    columns = jnp.where(lane == 0, peak, total)
    rows = jnp.concatenate([columns, jnp.zeros((HD - ROWS, HD), F32)], axis=0).T
    pack(out_ref, weighted, rows[0:1], rows[1:2])


def project_decode(at, phase, ratio, length, p_own, p_other, weights, queries, res_k, res_v, tails):
    here = lambda array: pltpu.with_memory_space_constraint(array, pltpu.VMEM)
    far = lambda array: pltpu.with_memory_space_constraint(array, pltpu.HBM)
    scalar, vmem = pl.BlockSpec(memory_space=pltpu.SMEM), pl.BlockSpec(memory_space=pltpu.VMEM)
    hbm = pl.BlockSpec(memory_space=pltpu.HBM)
    return pl.pallas_call(
        decode_kernel,
        out_shape=(
            pltpu.VMEM((REQ, NB, HD), BF),
            pltpu.VMEM((REQ, NB, HD), BF),
            pltpu.VMEM((8, ROWS + 16, HD), BF),
        ),
        in_specs=[scalar] * 4 + [vmem, hbm, hbm] + [vmem] * 4,
        out_specs=(vmem, vmem, vmem),
        scratch_shapes=[
            pltpu.VMEM((8, 8, HD, 2 * HD), BF),
            pltpu.VMEM((4, REQ * NB, G * HD), BF),
            pltpu.SemaphoreType.DMA((8,)),
            pltpu.SemaphoreType.DMA((4,)),
        ],
        compiler_params=pltpu.CompilerParams(vmem_limit_bytes=40 << 20),
        name="project_decode",
    )(
        at,
        phase,
        ratio,
        length,
        here(p_own),
        far(p_other),
        far(weights),
        here(queries),
        here(res_k),
        here(res_v),
        here(tails),
    )


def combine_kernel(in_ref, out_ref):
    pack(out_ref, *merge(in_ref, False))


def combine(state):
    return pl.pallas_call(
        combine_kernel, out_shape=pltpu.VMEM(state.shape, BF), name="combine"
    )(pltpu.with_memory_space_constraint(state, pltpu.VMEM))


def attend_kernel(in_ref, w_ref, out_ref):
    attended, _, _ = merge(in_ref, True)
    rows = STEPS * REQ
    flat = jnp.concatenate([attended[g * rows : (g + 1) * rows] for g in range(G)], axis=1)
    part = dot_nn(flat.astype(BF), w_ref[...])
    high = part.astype(BF)
    both = jnp.concatenate([high.astype(F32), part - high.astype(F32)], axis=0).astype(BF)
    for copy in range(8):
        out_ref[copy] = both


def attend(state, out_weight):
    return pl.pallas_call(
        attend_kernel,
        out_shape=pltpu.VMEM((8, 2 * STEPS * REQ, HD), BF),
        name="attend",
    )(
        pltpu.with_memory_space_constraint(state, pltpu.VMEM),
        pltpu.with_memory_space_constraint(out_weight, pltpu.VMEM),
    )


def total_kernel(in_ref, out_ref):
    rows = STEPS * REQ
    both = jnp.sum(in_ref[...].astype(F32), axis=0)
    out_ref[...] = (both[:rows] + both[rows:]).astype(BF)


def total(parts):
    return pl.pallas_call(
        total_kernel, out_shape=jax.ShapeDtypeStruct((STEPS * REQ, HD), BF), name="total"
    )(pltpu.with_memory_space_constraint(parts, pltpu.VMEM))


def lines(axes):
    def device(z, y, x, c):
        return ((z * 8 + y) * 4 + x) * 2 + c

    return [
        [device(i, j, x, c) if axes[c] == "z" else device(j, i, x, c) for i in range(8)]
        for c in range(2)
        for x in range(4)
        for j in range(8)
    ]


def body(
    raw_keys,
    raw_values,
    phase,
    ratio,
    resident_len,
    beacon_queries,
    beacon_wk,
    beacon_wv,
    resident_keys,
    resident_values,
    decode_queries,
    out_weight,
):
    shard = lax.axis_index(SEQ)
    count = lax.axis_size(SEQ)
    raw_k, raw_v = raw_keys[:, :, 0], raw_values[:, :, 0]
    staged = stage(beacon_wk, beacon_wv)
    tails = tail(raw_k, raw_v)
    column = lax.all_to_all(staged, ALL, 0, 0, axis_index_groups=lines("yz"))
    column = column.reshape(8 * HD, 2 * HD)
    at = jnp.stack([shard, lax.axis_index("c"), (shard == count - 1).astype(jnp.int32)])
    queries = jnp.transpose(beacon_queries[:, :, 0], (0, 2, 1, 3))
    sums, stats = pool_own(at, phase, ratio, queries, raw_k, raw_v)
    column, sums, stats, tails = lax.optimization_barrier((column, sums, stats, tails))
    near = lax.ppermute(tails, SEQ, [(i, i + 1) for i in range(count - 1)])
    weights = lax.all_gather(column, ALL, axis=0, tiled=True, axis_index_groups=lines("zy"))
    weights = weights.reshape(8, 8, HD, 2 * HD)
    pooled = pool_rest(at, phase, ratio, queries, near, sums, stats)
    p_own = lax.all_to_all(pooled, "x", 0, 0)
    p_other = lax.ppermute(p_own, "c", [(0, 1), (1, 0)])
    step_queries = jnp.transpose(decode_queries[:, :, 0], (2, 0, 1, 3)).reshape(ROWS, HD)
    beacon_k, beacon_v, state = project_decode(
        at,
        phase,
        ratio,
        resident_len,
        p_own,
        p_other,
        weights,
        step_queries,
        resident_keys[:, :, 0],
        resident_values[:, :, 0],
        tails,
    )
    state = combine(lax.all_to_all(state, ALL, 0, 0, axis_index_groups=lines("yz")))
    parts = attend(lax.all_to_all(state, ALL, 0, 0, axis_index_groups=lines("zy")), out_weight)
    parts = lax.all_to_all(parts, ("x", "c"), 0, 0)
    projected = total(parts).reshape(STEPS, REQ, HD)
    return beacon_k[:, :, None], beacon_v[:, :, None], projected


def solution(mesh):
    fine = Mesh(mesh.devices.reshape(8, 8, 4, 2), ("z", "y", "x", "c"))
    head = ("x", "c")
    return jax.shard_map(
        body,
        mesh=fine,
        in_specs=(
            P(None, SEQ, head, None),
            P(None, SEQ, head, None),
            P(),
            P(),
            P(),
            P(None, SEQ, head, None, None),
            P(SEQ, head),
            P(SEQ, head),
            P(None, SEQ, head, None),
            P(None, SEQ, head, None),
            P(None, None, head, None, None),
            P(head, SEQ),
        ),
        out_specs=(
            P(None, SEQ, head, None),
            P(None, SEQ, head, None),
            P(None, None, SEQ),
        ),
        check_vma=False,
    )
```
